512 devices in a mesh: seq: 32 (over z, core), mp: 16 (over y, x).
Axes of the slice: x: 4, y: 4, z: 16, core: 2. Of those that a mesh axis runs over, the one named last changes fastest.
Arguments:
- residual: bfloat16 [4096, 8192], P('seq', 'mp'), may hold values from -6 to 6
- hyena_streams: bfloat16 [4096, 3, 8192], P('seq', None, 'mp'), may hold values from -6 to 6
- hyena_filter: float32 [7, 8192], P(None, 'mp'), may hold values from -3 to 3
- attention_streams: bfloat16 [4096, 3, 8192], P('seq', None, 'mp'), may hold values from -4.5 to 4.5
- norm_gain: float32 [8192], P('mp'), may hold values from 0.5 to 1.5
- record_starts: int32 [16], replicated, may hold values from 0 to 4095, as said below
- record_lengths: int32 [16], replicated, may hold values from 1 to 2048, as said below
- segment_ids: int32 [4096], P('seq'), may hold values from 0 to 15, as said below
Outputs:
- mixed: float32 [4096, 8192], P('seq', 'mp')
- record_energy: float32 [16], replicated
The draws below stay inside these ranges and needn't reach their ends.
Inputs may be any that keep to these rules, and one draw needn't show every extreme that they name: Records lie end to end from position 0: record_starts[r] is the sum of record_lengths of the records before r, and they cover all 4096 positions; one record has exactly 2048 positions. record_starts[r] is the first position of record r, rising with r. segment_ids[t] is the record r with record_starts[r] <= t < record_starts[r] + record_lengths[r].
All inputs are finite; a program needn't handle non-finite values.
Results may differ from the reference program's by a relative error of at most 0.0005.
Values may be sent and summed in bfloat16 or wider, within the bound.
No kernel may reach another device: no remote copies, remote signals or barrier semaphores. Data moves between devices by JAX's collectives and lax.ppermute only.
A program may use at most 64 MiB of HBM per device.

```python
import jax
import jax.numpy as jnp
from jax import lax

D = 8192
HEADS = 64
HEAD_DIM = 128
TAPS = 7
RECORDS = 16
LENGTH = 4096


def record_layout(key):
    key_weights, key_place = jax.random.split(key)
    weights = jax.random.randint(key_weights, (RECORDS - 1,), 1, 9)
    rest = LENGTH - LENGTH // 2
    parts = rest * weights // jnp.sum(weights)
    parts = parts.at[RECORDS - 2].add(rest - jnp.sum(parts))
    place = jax.random.randint(key_place, (), 0, RECORDS)
    index = jnp.arange(RECORDS)
    before = jnp.clip(index - 1, 0, RECORDS - 2)
    same = jnp.clip(index, 0, RECORDS - 2)
    lengths = jnp.where(index < place, parts[same], jnp.where(index == place, LENGTH // 2, parts[before]))
    starts = jnp.cumsum(lengths) - lengths
    return (starts.astype(jnp.int32), lengths.astype(jnp.int32))


def draw_record_starts(key, part):
    starts, lengths = record_layout(key)
    return starts


def draw_record_lengths(key, part):
    starts, lengths = record_layout(key)
    return lengths


def draw_segment_ids(key, part):
    starts, lengths = record_layout(key)
    positions = jnp.arange(LENGTH, dtype=jnp.int32)
    inside = (positions[:, None] >= starts[None, :]).astype(jnp.int32)
    return (jnp.sum(inside, axis=1) - 1).astype(jnp.int32)


def draw_attention_streams(key, part):
    key = jax.random.fold_in(key, 11)
    result = jnp.clip(jax.random.normal(key, (LENGTH, 3, D), jnp.float32), -4.5, 4.5)
    return result.astype(jnp.bfloat16)


def steps_of(stream_key, dims, shards, least, top_value):
    factor_of = 1.0
    for dim, shards_of in shards:
        steps = jax.random.uniform(jax.random.fold_in(jax.random.fold_in(stream_key, 6), dim), (shards_of,), jnp.float32, least / len(shards), top_value / len(shards))
        factor_of = factor_of * jnp.repeat(jnp.exp(steps), dims[dim] // shards_of).reshape((-1,) + (1,) * (len(dims) - 1 - dim))
    return factor_of


def gaussian(rng, extent, spread, most, cuts=(), kind=jnp.bfloat16):
    values = jax.random.normal(rng, extent, jnp.float32) * spread
    if len(cuts) > 0:
        values = steps_of(rng, extent, cuts, -0.22, 0.18) * values
    return jnp.clip(values, min=-most, max=most).astype(kind)


def setup_inputs(seed: int = 0) -> dict:
    splits = jax.random.split(jax.random.key(seed), 9)
    residual = gaussian(splits[0], (LENGTH, D), 1.0, 6.0, ((0, 32), (1, 16)))
    hyena_streams = gaussian(splits[1], (LENGTH, 3, D), 1.0, 6.0, ((0, 32), (2, 16)))
    hyena_filter = gaussian(splits[2], (TAPS, D), 0.5, 3.0, ((1, 16),), jnp.float32)
    attention_streams = draw_attention_streams(jax.random.fold_in(splits[8], 71), 0)
    norm_gain = jnp.clip(1.0 + 0.1 * jax.random.normal(splits[4], (D,), jnp.float32), 0.5, 1.5)
    record_starts = draw_record_starts(jax.random.fold_in(splits[8], 71), 0)
    record_lengths = draw_record_lengths(jax.random.fold_in(splits[8], 71), 0)
    segment_ids = draw_segment_ids(jax.random.fold_in(splits[8], 71), 0)
    return dict(residual=residual, hyena_streams=hyena_streams, hyena_filter=hyena_filter, attention_streams=attention_streams, norm_gain=norm_gain, record_starts=record_starts, record_lengths=record_lengths, segment_ids=segment_ids)


def reference(residual, hyena_streams, hyena_filter, attention_streams, norm_gain, record_starts, record_lengths, segment_ids):
    positions = jnp.arange(LENGTH, dtype=jnp.int32)
    row_start = record_starts[segment_ids].astype(jnp.int32)
    product = hyena_streams[:, 1].astype(jnp.float32) * hyena_streams[:, 2].astype(jnp.float32)
    padded = jnp.concatenate([jnp.zeros((TAPS - 1, D), jnp.float32), product], axis=0)
    filtered = jnp.zeros((LENGTH, D), jnp.float32)
    for tap in range(TAPS):
        term = padded[TAPS - 1 - tap:TAPS - 1 - tap + LENGTH]
        valid = (positions - tap >= row_start)[:, None]
        filtered = filtered + jnp.where(valid, hyena_filter[tap][None, :] * term, jnp.float32(0.0))
    hyena_out = hyena_streams[:, 0].astype(jnp.float32) * filtered
    allowed = (positions[None, :] <= positions[:, None]) & (positions[None, :] >= row_start[:, None])
    query = attention_streams[:, 0].reshape(LENGTH, HEADS, HEAD_DIM).transpose(1, 0, 2)
    keys = attention_streams[:, 1].reshape(LENGTH, HEADS, HEAD_DIM).transpose(1, 0, 2)
    values = attention_streams[:, 2].reshape(LENGTH, HEADS, HEAD_DIM).transpose(1, 0, 2)
    scale = HEAD_DIM ** (-0.5)

    def one_head(operands):
        q_head, k_head, v_head = operands
        scores = jnp.dot(q_head, k_head.T, preferred_element_type=jnp.float32) * scale
        masked = jnp.where(allowed, scores, jnp.float32(-1e+30))
        top = lax.optimization_barrier(jnp.max(masked, axis=1, keepdims=True))
        weights = jnp.where(allowed, jnp.exp(scores - top), jnp.float32(0.0))
        totals = lax.optimization_barrier(jnp.sum(weights, axis=1, keepdims=True))
        summed = jnp.dot(weights.astype(jnp.bfloat16), v_head, preferred_element_type=jnp.float32)
        return summed / totals
    heads_out = lax.map(one_head, (query, keys, values))
    attention_out = heads_out.transpose(1, 0, 2).reshape(LENGTH, D)
    stream = residual.astype(jnp.float32) + hyena_out + attention_out
    mean_square = lax.optimization_barrier(jnp.mean(stream * stream, axis=1))
    mixed = stream * lax.rsqrt(mean_square + 1e-05)[:, None] * norm_gain[None, :]
    table = segment_ids[:, None] == jnp.arange(RECORDS, dtype=jnp.int32)[None, :]
    record_sum = lax.optimization_barrier(jnp.sum(jnp.where(table, mean_square[:, None], jnp.float32(0.0)), axis=0))
    record_energy = record_sum / record_lengths.astype(jnp.float32)
    return (mixed, record_energy)
```

```python
import functools

import jax
import jax.numpy as jnp
from jax import lax
from jax.experimental import pallas as pl
from jax.experimental.pallas import tpu as pltpu
from jax.sharding import Mesh
from jax.sharding import PartitionSpec as P

D = 8192
HEAD_DIM = 128
GROUP = 4
GROUPS = 4
MASKED = -1e30
SCALE = HEAD_DIM**-0.5 * 1.4426950408889634
POSITIONS = ("zg", "zl", "core")


def pack_kernel(x_ref, out_ref):
    for head in range(GROUP):
        for stream in range(3):
            out_ref[head, stream] = x_ref[stream, :, head * HEAD_DIM : (head + 1) * HEAD_DIM]


def pack(streams):
    rows = streams.shape[1]
    return pl.pallas_call(
        pack_kernel,
        out_shape=jax.ShapeDtypeStruct((GROUP, 3, rows, HEAD_DIM), streams.dtype),
        name="pack_heads",
    )(streams)


def attend_kernel(back, first, last, scalars, starts, *refs):
    if first:
        q_ref, other_ref = refs[:2]
        own_ref, own_offset = q_ref, 1
        state_in, rest = None, refs[2:]
    else:
        q_ref, own_ref, other_ref = refs[:3]
        own_offset = 0
        state_in, rest = refs[3:6], refs[6:]
    group, core = scalars[0], scalars[1]
    rows = q_ref.shape[2]
    for block in range(GROUP):
        q = q_ref[block, 0]
        query_pos = ((group * GROUP + block) * 2 + core) * rows + lax.broadcasted_iota(
            jnp.int32, (rows, 1), 0
        )
        row_start = jnp.zeros((rows, 1), jnp.int32)
        for record in range(starts.shape[0]):
            here = starts[record]
            row_start = jnp.where(query_pos >= here, here, row_start)
        if back == 0:
            low, high = 0, block + 1
        elif back == 1:
            low, high = 0, GROUP
        else:
            low, high = block, GROUP
        count = (high - low) * rows
        scores = []
        sides = ((own_ref, own_offset, core), (other_ref, 0, 1 - core))
        for ref, offset, key_core in sides:
            keys = ref[low:high, offset].reshape(count, HEAD_DIM)
            s = lax.dot_general(q, keys, (((1,), (1,)), ((), ())), preferred_element_type=jnp.float32)
            place = lax.broadcasted_iota(jnp.int32, (1, count), 1)
            key_block = place // rows + low
            key_pos = (((group - back) * GROUP + key_block) * 2 + key_core) * rows + place % rows
            allowed = key_pos >= row_start
            if back == 0:
                allowed = allowed & (key_pos <= query_pos)
            scores.append(jnp.where(allowed, s * SCALE, MASKED))
        top = jnp.maximum(
            jnp.max(scores[0], axis=1, keepdims=True), jnp.max(scores[1], axis=1, keepdims=True)
        )
        if state_in is not None:
            top = jnp.maximum(top, state_in[0][block])
        total = jnp.zeros((rows, 1), jnp.float32)
        summed = jnp.zeros((rows, HEAD_DIM), jnp.float32)
        for s, (ref, offset, _) in zip(scores, sides):
            weights = jnp.exp2(s - top)
            total = total + jnp.sum(weights, axis=1, keepdims=True)
            values = ref[low:high, offset + 1].reshape(count, HEAD_DIM)
            summed = summed + jnp.dot(
                weights.astype(jnp.bfloat16), values, preferred_element_type=jnp.float32
            )
        if state_in is not None:
            factor = jnp.exp2(state_in[0][block] - top)
            total = total + state_in[1][block] * factor
            summed = summed + state_in[2][block] * factor
        if last:
            rest[0][block] = summed / total
        else:
            rest[0][block] = top
            rest[1][block] = total
            rest[2][block] = summed


def attend(back, scalars, starts, received, own, other, state):
    rows = received.shape[2]
    first, last = state is None, back == 2
    smem = pl.BlockSpec(memory_space=pltpu.SMEM)
    vmem = pl.BlockSpec(memory_space=pltpu.VMEM)
    column = jax.ShapeDtypeStruct((GROUP, rows, 1), jnp.float32)
    full = jax.ShapeDtypeStruct((GROUP, rows, HEAD_DIM), jnp.float32)
    operands = (scalars, starts, received) + ((other,) if first else (own, other) + tuple(state))
    out_shape = full if last else (column, column, full)
    return pl.pallas_call(
        functools.partial(attend_kernel, back, first, last),
        out_shape=out_shape,
        in_specs=[smem, smem] + [vmem] * (len(operands) - 2),
        out_specs=vmem if last else (vmem, vmem, vmem),
        compiler_params=pltpu.CompilerParams(vmem_limit_bytes=32 * 1024 * 1024),
        cost_estimate=pl.CostEstimate(
            flops=4 * GROUP * rows * GROUP * 2 * rows * HEAD_DIM,
            bytes_accessed=4 * 1024 * 1024,
            transcendentals=GROUP * rows * GROUP * 2 * rows,
        ),
        name=f"attend_back{back}",
    )(*operands)


def on_device(
    residual,
    hyena_streams,
    hyena_filter,
    attention_streams,
    norm_gain,
    record_starts,
    record_lengths,
    segment_ids,
):
    rows, width = residual.shape
    taps = hyena_filter.shape[0]
    records = record_starts.shape[0]
    group, core = lax.axis_index("zg"), lax.axis_index("core")
    scalars = jnp.stack([group, core]).astype(jnp.int32)

    with jax.named_scope("heads_to_chips"):
        packed = pack(attention_streams.transpose(1, 0, 2))
        received = lax.all_to_all(packed, "zl", 0, 0, tiled=True)
    key_value = received[:, 1:]
    swap = [(0, 1), (1, 0)]
    with jax.named_scope("keys_values_from_before"):
        before1 = lax.ppermute(key_value, "zg", [(i, i + 1) for i in range(GROUPS - 1)])
        before2 = lax.ppermute(key_value, "zg", [(i, i + 2) for i in range(GROUPS - 2)])
        other0 = lax.ppermute(key_value, "core", swap)
        other1 = lax.ppermute(before1, "core", swap)
        other2 = lax.ppermute(before2, "core", swap)

    with jax.named_scope("hyena"):
        edge, _ = lax.optimization_barrier((hyena_streams[rows - (taps - 1) :, 1:3, :], received))
        seq = lax.axis_size(POSITIONS)
        rim = lax.ppermute(edge, POSITIONS, [(i, i + 1) for i in range(seq - 1)])
        positions = lax.axis_index(POSITIONS) * rows + jnp.arange(rows, dtype=jnp.int32)
        table = segment_ids[:, None] == jnp.arange(records, dtype=jnp.int32)[None, :]
        row_start = jnp.sum(jnp.where(table, record_starts[None, :], 0), axis=1)
        product = hyena_streams[:, 1].astype(jnp.float32) * hyena_streams[:, 2].astype(jnp.float32)
        rim_product = rim[:, 0].astype(jnp.float32) * rim[:, 1].astype(jnp.float32)
        padded = jnp.concatenate([rim_product, product], axis=0)
        filtered = jnp.zeros((rows, width), jnp.float32)
        for tap in range(taps):
            term = padded[taps - 1 - tap : taps - 1 - tap + rows]
            valid = (positions - tap >= row_start)[:, None]
            filtered = filtered + jnp.where(
                valid, hyena_filter[tap][None, :] * term, jnp.float32(0.0)
            )
        hyena_out = hyena_streams[:, 0].astype(jnp.float32) * filtered
        base = residual.astype(jnp.float32) + hyena_out

    with jax.named_scope("attention"):
        state = attend(0, scalars, record_starts, received, None, other0, None)
        state = attend(1, scalars, record_starts, received, before1, other1, state)
        out = attend(2, scalars, record_starts, received, before2, other2, state)
        heads = lax.all_to_all(out, "zl", 0, 0, tiled=True)

    stream = base + heads.transpose(1, 0, 2).reshape(rows, width)
    with jax.named_scope("mean_square"):
        squares = jnp.sum(stream * stream, axis=1)
        size = lax.axis_size("mp")
        parts = lax.all_to_all(jnp.broadcast_to(squares, (size, 1, rows)), "mp", 0, 0, tiled=True)
        mean_square = jnp.sum(parts, axis=(0, 1)) / D
    mixed = stream * lax.rsqrt(mean_square + 1e-05)[:, None] * norm_gain[None, :]
    with jax.named_scope("record_energy"):
        local_sums = jnp.sum(jnp.where(table, mean_square[:, None], jnp.float32(0.0)), axis=0)
        parts = jnp.broadcast_to(jnp.pad(local_sums, (0, 128 - records)), (seq, 1, 128))
        parts = lax.all_to_all(parts, POSITIONS, 0, 0, tiled=True)
        record_sum = jnp.sum(parts, axis=(0, 1))[:records]
        record_energy = record_sum / record_lengths.astype(jnp.float32)
    return (mixed, record_energy)


def solution(mesh):
    fine = Mesh(
        mesh.devices.reshape(GROUPS, GROUP, 2, mesh.shape["mp"]), ("zg", "zl", "core", "mp")
    )
    return jax.shard_map(
        on_device,
        mesh=fine,
        in_specs=(
            P(POSITIONS, "mp"),
            P(POSITIONS, None, "mp"),
            P(None, "mp"),
            P(POSITIONS, None, "mp"),
            P("mp"),
            P(),
            P(),
            P(POSITIONS),
        ),
        out_specs=(P(POSITIONS, "mp"), P()),
        check_vma=False,
    )
```

```python
import functools

import jax
import jax.numpy as jnp
from jax import lax
from jax.experimental import pallas as pl
from jax.experimental.pallas import tpu as pltpu
from jax.sharding import Mesh
from jax.sharding import PartitionSpec as P

D = 8192
HEAD_DIM = 128
GROUP = 4
GROUPS = 4
MASKED = -1e30
SCALE = HEAD_DIM**-0.5 * 1.4426950408889634
POSITIONS = ("zg", "zl", "core")


def pack_kernel(x_ref, out_ref):
    for head in range(GROUP):
        for stream in range(3):
            out_ref[head, stream] = x_ref[stream, :, head * HEAD_DIM : (head + 1) * HEAD_DIM]


def pack(streams):
    rows = streams.shape[1]
    return pl.pallas_call(
        pack_kernel,
        out_shape=jax.ShapeDtypeStruct((GROUP, 3, rows, HEAD_DIM), streams.dtype),
        name="pack_heads",
    )(streams)


def attend_kernel(back, first, last, scalars, starts, *refs):
    if first:
        q_ref, other_ref = refs[:2]
        own_ref, own_offset = q_ref, 1
        state_in, rest = None, refs[2:]
    else:
        q_ref, own_ref, other_ref = refs[:3]
        own_offset = 0
        state_in, rest = refs[3:6], refs[6:]
    group, core = scalars[0], scalars[1]
    rows = q_ref.shape[2]
    for block in range(GROUP):
        q = q_ref[block, 0]
        query_pos = ((group * GROUP + block) * 2 + core) * rows + lax.broadcasted_iota(
            jnp.int32, (rows, 1), 0
        )
        row_start = row_starts(starts, query_pos)
        if back == 0:
            low, high = 0, block + 1
        elif back == 1:
            low, high = 0, GROUP
        else:
            low, high = block, GROUP
        count = (high - low) * rows
        scores = []
        sides = ((own_ref, own_offset, core), (other_ref, 0, 1 - core))
        for ref, offset, key_core in sides:
            keys = ref[low:high, offset].reshape(count, HEAD_DIM)
            s = lax.dot_general(q, keys, (((1,), (1,)), ((), ())), preferred_element_type=jnp.float32)
            place = lax.broadcasted_iota(jnp.int32, (1, count), 1)
            key_block = place // rows + low
            key_pos = (((group - back) * GROUP + key_block) * 2 + key_core) * rows + place % rows
            allowed = key_pos >= row_start
            if back == 0:
                allowed = allowed & (key_pos <= query_pos)
            scores.append(jnp.where(allowed, s * SCALE, MASKED))
        top = jnp.maximum(
            jnp.max(scores[0], axis=1, keepdims=True), jnp.max(scores[1], axis=1, keepdims=True)
        )
        if state_in is not None:
            top = jnp.maximum(top, state_in[0][block])
        total = jnp.zeros((rows, 1), jnp.float32)
        summed = jnp.zeros((rows, HEAD_DIM), jnp.float32)
        for s, (ref, offset, _) in zip(scores, sides):
            weights = jnp.exp2(s - top)
            total = total + jnp.sum(weights, axis=1, keepdims=True)
            values = ref[low:high, offset + 1].reshape(count, HEAD_DIM)
            summed = summed + jnp.dot(
                weights.astype(jnp.bfloat16), values, preferred_element_type=jnp.float32
            )
        if state_in is not None:
            factor = jnp.exp2(state_in[0][block] - top)
            total = total + state_in[1][block] * factor
            summed = summed + state_in[2][block] * factor
        if last:
            rest[0][block] = summed / total
        else:
            rest[0][block] = top
            rest[1][block] = total
            rest[2][block] = summed


def attend(back, scalars, starts, received, own, other, state):
    rows = received.shape[2]
    first, last = state is None, back == 2
    smem = pl.BlockSpec(memory_space=pltpu.SMEM)
    vmem = pl.BlockSpec(memory_space=pltpu.VMEM)
    column = jax.ShapeDtypeStruct((GROUP, rows, 1), jnp.float32)
    full = jax.ShapeDtypeStruct((GROUP, rows, HEAD_DIM), jnp.float32)
    operands = (scalars, starts, received) + ((other,) if first else (own, other) + tuple(state))
    out_shape = full if last else (column, column, full)
    return pl.pallas_call(
        functools.partial(attend_kernel, back, first, last),
        out_shape=out_shape,
        in_specs=[smem, smem] + [vmem] * (len(operands) - 2),
        out_specs=vmem if last else (vmem, vmem, vmem),
        compiler_params=pltpu.CompilerParams(vmem_limit_bytes=32 * 1024 * 1024),
        cost_estimate=cost(2500),
        name=f"attend_back{back}",
    )(*operands)


def row_starts(starts, positions):
    found = jnp.zeros_like(positions)
    for record in range(starts.shape[0]):
        here = starts[record]
        found = jnp.where(positions >= here, here, found)
    return found


def hyena_kernel(scalars, starts, residual, streams, rim, taps_ref, out_ref, padded):
    rows = residual.shape[0]
    edge = rim.shape[1]
    taps = taps_ref.shape[0]
    positions = scalars[2] * rows + lax.broadcasted_iota(jnp.int32, (rows, 1), 0)
    first = row_starts(starts, positions)
    padded[:edge] = rim[0].astype(jnp.float32) * rim[1].astype(jnp.float32)
    padded[edge:] = streams[1].astype(jnp.float32) * streams[2].astype(jnp.float32)
    filtered = jnp.zeros(out_ref.shape, jnp.float32)
    for tap in range(taps):
        term = taps_ref[tap : tap + 1, :] * padded[edge - tap : edge - tap + rows]
        filtered = filtered + jnp.where(positions - tap >= first, term, 0.0)
    out_ref[...] = residual[...].astype(jnp.float32) + streams[0].astype(jnp.float32) * filtered


def stream_kernel(base, heads, stream_ref, squares_ref):
    rows = base.shape[0]
    squares = jnp.zeros((rows, HEAD_DIM), jnp.float32)
    for head in range(GROUP):
        columns = slice(head * HEAD_DIM, (head + 1) * HEAD_DIM)
        value = base[:, columns] + heads[head]
        stream_ref[:, columns] = value
        squares = squares + value * value
    line = jnp.sum(squares.T, axis=0, keepdims=True)
    for device in range(squares_ref.shape[0]):
        squares_ref[device] = line


def records_kernel(scalars, starts, lengths, parts, mean_ref, sums_ref):
    rows = parts.shape[2]
    line = jnp.sum(parts[:, 0, :], axis=0, keepdims=True) / D
    mean = jnp.broadcast_to(line, (rows, rows)).T
    mean_ref[...] = mean
    position = scalars[2] * rows + lax.broadcasted_iota(jnp.int32, (rows, rows), 0)
    first = starts[...]
    inside = (position >= first) & (position < first + lengths[...])
    sums = jnp.sum(jnp.where(inside, mean, 0.0), axis=0, keepdims=True)
    for device in range(sums_ref.shape[0]):
        sums_ref[device] = sums


def scale_kernel(stream, mean, gain, out_ref):
    factor = lax.rsqrt(mean[...] + 1e-05)
    for head in range(GROUP):
        columns = slice(head * HEAD_DIM, (head + 1) * HEAD_DIM)
        out_ref[:, columns] = stream[:, columns] * factor * gain[:, columns]


SMEM = pl.BlockSpec(memory_space=pltpu.SMEM)
VMEM = pl.BlockSpec(memory_space=pltpu.VMEM)


def cost(nanoseconds):
    return pl.CostEstimate(flops=nanoseconds * 1_000_000, bytes_accessed=1 << 20, transcendentals=0)


def on_device(
    residual,
    hyena_streams,
    hyena_filter,
    attention_streams,
    norm_gain,
    record_starts,
    record_lengths,
    segment_ids,
):
    rows, width = residual.shape
    records = record_starts.shape[0]
    group, core = lax.axis_index("zg"), lax.axis_index("core")
    seq, mp = lax.axis_size(POSITIONS), lax.axis_size("mp")
    scalars = jnp.stack([group, core, lax.axis_index(POSITIONS)]).astype(jnp.int32)

    with jax.named_scope("heads_to_chips"):
        packed = pack(attention_streams.transpose(1, 0, 2))
        received = lax.all_to_all(packed, "zl", 0, 0, tiled=True)
    key_value = received[:, 1:]
    swap = [(0, 1), (1, 0)]
    with jax.named_scope("keys_values_from_before"):
        before1 = lax.ppermute(key_value, "zg", [(i, i + 1) for i in range(GROUPS - 1)])
        before2 = lax.ppermute(key_value, "zg", [(i, i + 2) for i in range(GROUPS - 2)])
        other0 = lax.ppermute(key_value, "core", swap)
        other1 = lax.ppermute(before1, "core", swap)

    with jax.named_scope("hyena"):
        streams = hyena_streams.transpose(1, 0, 2)
        edge, _ = lax.optimization_barrier((streams[1:, rows - 16 :], other0))
        rim = lax.ppermute(edge, POSITIONS, [(i, i + 1) for i in range(seq - 1)])
        base = pl.pallas_call(
            hyena_kernel,
            out_shape=jax.ShapeDtypeStruct((rows, width), jnp.float32),
            in_specs=[SMEM, SMEM, VMEM, VMEM, VMEM, VMEM],
            out_specs=VMEM,
            scratch_shapes=[pltpu.VMEM((rows + 16, width), jnp.float32)],
            cost_estimate=cost(1500),
            name="hyena",
        )(scalars, record_starts, residual, streams, rim, hyena_filter)

    with jax.named_scope("attention"):
        state = attend(0, scalars, record_starts, received, None, other0, None)
        before2, base, state = lax.optimization_barrier((before2, base, state))
        other2 = lax.ppermute(before2, "core", swap)
        state = attend(1, scalars, record_starts, received, before1, other1, state)
        out = attend(2, scalars, record_starts, received, before2, other2, state)
        heads = lax.all_to_all(out, "zl", 0, 0, tiled=True)

    with jax.named_scope("mean_square"):
        stream, squares = pl.pallas_call(
            stream_kernel,
            out_shape=(
                jax.ShapeDtypeStruct((rows, width), jnp.float32),
                jax.ShapeDtypeStruct((mp, 1, rows), jnp.float32),
            ),
            name="stream",
        )(base, heads)
        parts = lax.all_to_all(squares, "mp", 0, 0, tiled=True)
    with jax.named_scope("record_energy"):
        lines = [jnp.pad(x, (0, 128 - records))[None, :] for x in (record_starts, record_lengths)]
        mean, sums = pl.pallas_call(
            records_kernel,
            out_shape=(
                jax.ShapeDtypeStruct((rows, rows), jnp.float32),
                jax.ShapeDtypeStruct((seq, 1, 128), jnp.float32),
            ),
            in_specs=[SMEM, VMEM, VMEM, VMEM],
            name="records",
        )(scalars, *lines, parts)
        sums = lax.all_to_all(sums, POSITIONS, 0, 0, tiled=True)
        record_energy = jnp.sum(sums, axis=(0, 1))[:records] / record_lengths.astype(jnp.float32)
    mixed = pl.pallas_call(
        scale_kernel,
        out_shape=jax.ShapeDtypeStruct((rows, width), jnp.float32),
        cost_estimate=cost(1000),
        name="scale",
    )(stream, mean, norm_gain[None, :])
    return (mixed, record_energy)


def solution(mesh):
    fine = Mesh(
        mesh.devices.reshape(GROUPS, GROUP, 2, mesh.shape["mp"]), ("zg", "zl", "core", "mp")
    )
    return jax.shard_map(
        on_device,
        mesh=fine,
        in_specs=(
            P(POSITIONS, "mp"),
            P(POSITIONS, None, "mp"),
            P(None, "mp"),
            P(POSITIONS, None, "mp"),
            P("mp"),
            P(),
            P(),
            P(POSITIONS),
        ),
        out_specs=(P(POSITIONS, "mp"), P()),
        check_vma=False,
    )
```

```python
import functools

import jax
import jax.numpy as jnp
from jax import lax
from jax.experimental import pallas as pl
from jax.experimental.pallas import tpu as pltpu
from jax.sharding import Mesh
from jax.sharding import PartitionSpec as P

D = 8192
HEAD_DIM = 128
GROUP = 4
MASKED = -1e30
SCALE = HEAD_DIM**-0.5 * 1.4426950408889634
POSITIONS = ("z", "core")
CHIPS = 16
LONG = 2048
SMEM = pl.BlockSpec(memory_space=pltpu.SMEM)
VMEM = pl.BlockSpec(memory_space=pltpu.VMEM)


def cost(nanoseconds):
    return pl.CostEstimate(flops=nanoseconds * 1_000_000, bytes_accessed=1 << 20, transcendentals=0)


def pack_kernel(x_ref, out_ref):
    for head in range(GROUP):
        for stream in range(3):
            out_ref[head, stream] = x_ref[stream, :, head * HEAD_DIM : (head + 1) * HEAD_DIM]


def pack(streams):
    rows = streams.shape[1]
    return pl.pallas_call(
        pack_kernel,
        out_shape=jax.ShapeDtypeStruct((GROUP, 3, rows, HEAD_DIM), streams.dtype),
        name="pack_heads",
    )(streams)


def attend_rows(q, query_pos, row_start, sources, state):
    rows = q.shape[0]
    scores = []
    for keys, _, first in sources:
        s = lax.dot_general(q, keys, (((1,), (1,)), ((), ())), preferred_element_type=jnp.float32)
        key_pos = jnp.concatenate(
            [here + lax.broadcasted_iota(jnp.int32, (1, rows), 1) for here in first], axis=1
        )
        allowed = (key_pos >= row_start) & (key_pos <= query_pos)
        scores.append(jnp.where(allowed, s * SCALE, MASKED))
    top = functools.reduce(jnp.maximum, [jnp.max(s, axis=1, keepdims=True) for s in scores])
    if state is not None:
        top = jnp.maximum(top, state[0])
    total = jnp.zeros((rows, 1), jnp.float32)
    summed = jnp.zeros((rows, HEAD_DIM), jnp.float32)
    for s, (_, values, _) in zip(scores, sources):
        weights = jnp.exp2(s - top)
        total = total + jnp.sum(weights, axis=1, keepdims=True)
        summed = summed + jnp.dot(
            weights.astype(jnp.bfloat16), values, preferred_element_type=jnp.float32
        )
    if state is not None:
        factor = jnp.exp2(state[0] - top)
        total = total + state[1] * factor
        summed = summed + state[2] * factor
    return top, total, summed


def chip_position(cut, group, place, core, rows):
    chip = lax.rem(group * GROUP + place + (cut + 2 * CHIPS), CHIPS)
    return (chip * 2 + core) * rows


def blocks_of(ref, low, high, offset=0):
    rows = ref.shape[2]
    return [ref[low:high, offset + i].reshape((high - low) * rows, HEAD_DIM) for i in range(2)]


def attend_kernel(cut, phase, scalars, starts, q_ref, *refs):
    group, core = scalars[0], scalars[1]
    rows = q_ref.shape[2]
    place = lax.broadcasted_iota(jnp.int32, (rows, 1), 0)

    def positions(of_group, block, of_core):
        return chip_position(cut, of_group, block, of_core, rows)

    for block in range(GROUP):
        q = q_ref[block, 0]
        query_pos = positions(group, block, core) + place
        row_start = row_starts(starts, query_pos)
        if phase == 0:
            other_ref = refs[0]
            outs = refs[2:5]
            state = None
            sources = [
                (
                    *blocks_of(q_ref, 0, block + 1, 1),
                    [positions(group, i, core) for i in range(block + 1)],
                ),
                (
                    *blocks_of(other_ref, 0, block + 1),
                    [positions(group, i, 1 - core) for i in range(block + 1)],
                ),
            ]
        else:
            key_core = core if phase == 1 else 1 - core
            state = [ref[block] for ref in refs[1:4]]
            sources = [
                (
                    *blocks_of(refs[0], 0, GROUP),
                    [positions(group - 1, i, key_core) for i in range(GROUP)],
                )
            ]
        top, total, summed = attend_rows(q, query_pos, row_start, sources, state)
        if phase < 2:
            outs = refs[2:5] if phase == 0 else refs[4:7]
            outs[0][block], outs[1][block], outs[2][block] = top, total, summed
        else:
            back_ref, out_ref = refs[4:]
            if block == 0:
                far_top = jnp.broadcast_to(back_ref[rows : rows + 1], (rows, rows)).T[:, :1]
                joint = jnp.maximum(top, far_top)
                near, far = jnp.exp2(top - joint), jnp.exp2(far_top - joint)
                total = total * near + far
                summed = summed * near + back_ref[:rows] * far
            out_ref[block] = summed / total
    if phase == 0:
        other_ref, far_ref = refs[:2]
        away_ref = refs[5]
        query_pos = positions(group + 2, 0, core) + place
        sources = [
            (*blocks_of(q_ref, 0, GROUP, 1), [positions(group, i, core) for i in range(GROUP)]),
            (*blocks_of(other_ref, 0, GROUP), [positions(group, i, 1 - core) for i in range(GROUP)]),
        ]
        top, total, summed = attend_rows(
            far_ref[...], query_pos, row_starts(starts, query_pos), sources, None
        )
        away_ref[:rows] = summed / total
        column = jnp.broadcast_to(top + jnp.log2(total), (rows, rows))
        away_ref[rows:] = column.T[: away_ref.shape[0] - rows]


def attend(cut, phase, scalars, starts, received, *others):
    rows = received.shape[2]
    column = jax.ShapeDtypeStruct((GROUP, rows, 1), jnp.float32)
    full = jax.ShapeDtypeStruct((GROUP, rows, HEAD_DIM), jnp.float32)
    away = jax.ShapeDtypeStruct((rows + 8, HEAD_DIM), jnp.float32)
    out_shape = ((column, column, full, away), (column, column, full), full)[phase]
    return pl.pallas_call(
        functools.partial(attend_kernel, cut, phase),
        out_shape=out_shape,
        in_specs=[SMEM, SMEM] + [VMEM] * (1 + len(others)),
        compiler_params=pltpu.CompilerParams(vmem_limit_bytes=32 * 1024 * 1024),
        cost_estimate=cost(2000),
        name=f"attend{phase}",
    )(scalars, starts, received, *others)


def row_starts(starts, positions):
    found = jnp.zeros_like(positions)
    for record in range(starts.shape[0]):
        here = starts[record]
        found = jnp.where(positions >= here, here, found)
    return found


def hyena_kernel(scalars, starts, residual, streams, rim, taps_ref, out_ref, padded):
    rows = residual.shape[0]
    edge = rim.shape[1]
    taps = taps_ref.shape[0]
    positions = scalars[2] * rows + lax.broadcasted_iota(jnp.int32, (rows, 1), 0)
    first = row_starts(starts, positions)
    padded[:edge] = rim[0].astype(jnp.float32) * rim[1].astype(jnp.float32)
    padded[edge:] = streams[1].astype(jnp.float32) * streams[2].astype(jnp.float32)
    filtered = jnp.zeros(out_ref.shape, jnp.float32)
    for tap in range(taps):
        term = taps_ref[tap : tap + 1, :] * padded[edge - tap : edge - tap + rows]
        filtered = filtered + jnp.where(positions - tap >= first, term, 0.0)
    out_ref[...] = residual[...].astype(jnp.float32) + streams[0].astype(jnp.float32) * filtered


def stream_kernel(base, heads, stream_ref, squares_ref):
    rows = base.shape[0]
    squares = jnp.zeros((rows, HEAD_DIM), jnp.float32)
    for head in range(GROUP):
        columns = slice(head * HEAD_DIM, (head + 1) * HEAD_DIM)
        value = base[:, columns] + heads[head]
        stream_ref[:, columns] = value
        squares = squares + value * value
    line = jnp.sum(squares.T, axis=0, keepdims=True)
    for device in range(squares_ref.shape[0]):
        squares_ref[device] = line


def records_kernel(scalars, starts, lengths, parts, mean_ref, sums_ref):
    rows = parts.shape[2]
    line = jnp.sum(parts[:, 0, :], axis=0, keepdims=True) / D
    mean = jnp.broadcast_to(line, (rows, rows)).T
    mean_ref[...] = mean
    position = scalars[2] * rows + lax.broadcasted_iota(jnp.int32, (rows, rows), 0)
    first = starts[...]
    inside = (position >= first) & (position < first + lengths[...])
    sums = jnp.sum(jnp.where(inside, mean, 0.0), axis=0, keepdims=True)
    for device in range(sums_ref.shape[0]):
        sums_ref[device] = sums


def scale_kernel(stream, mean, gain, out_ref):
    factor = lax.rsqrt(mean[...] + 1e-05)
    for head in range(GROUP):
        columns = slice(head * HEAD_DIM, (head + 1) * HEAD_DIM)
        out_ref[:, columns] = stream[:, columns] * factor * gain[:, columns]


def mixers(cut, packed, residual, streams, taps, starts):
    rows, width = residual.shape
    seq = lax.axis_size(POSITIONS)
    chip, core = lax.axis_index("z"), lax.axis_index("core")
    group = lax.rem(chip + CHIPS - cut, CHIPS) // GROUP
    scalars = jnp.stack([group, core, lax.axis_index(POSITIONS)]).astype(jnp.int32)
    groups = [
        [(cut + GROUP * k + i) % CHIPS for i in range(GROUP)] for k in range(CHIPS // GROUP)
    ]
    swap = [(0, 1), (1, 0)]

    def along(value, chips):
        return lax.ppermute(value, "z", [(i, (i + chips) % CHIPS) for i in range(CHIPS)])

    received = lax.all_to_all(packed, "z", 0, 0, axis_index_groups=groups, tiled=True)
    far = along(received[0, 0], -2 * GROUP)
    key_value = received[:, 1:]
    before = along(key_value, GROUP)
    other = lax.ppermute(key_value, "core", swap)
    rim = lax.ppermute(streams[1:, rows - 16 :], POSITIONS, [(i, i + 1) for i in range(seq - 1)])
    base = pl.pallas_call(
        hyena_kernel,
        out_shape=jax.ShapeDtypeStruct((rows, width), jnp.float32),
        in_specs=[SMEM, SMEM, VMEM, VMEM, VMEM, VMEM],
        out_specs=VMEM,
        scratch_shapes=[pltpu.VMEM((rows + 16, width), jnp.float32)],
        cost_estimate=cost(2000),
        name="hyena",
    )(scalars, starts, residual, streams, rim, taps)
    *state, away = attend(cut, 0, scalars, starts, received, other, far)
    back = along(away, 2 * GROUP)
    before, base, state = lax.optimization_barrier((before, base, state))
    before_other = lax.ppermute(before, "core", swap)
    state = attend(cut, 1, scalars, starts, received, before, *state)
    out = attend(cut, 2, scalars, starts, received, before_other, *state, back)
    heads = lax.all_to_all(out, "z", 0, 0, axis_index_groups=groups, tiled=True)
    return base, heads


def on_device(
    residual,
    hyena_streams,
    hyena_filter,
    attention_streams,
    norm_gain,
    record_starts,
    record_lengths,
    segment_ids,
):
    rows, width = residual.shape
    records = record_starts.shape[0]
    seq, mp = lax.axis_size(POSITIONS), lax.axis_size("mp")
    place = lax.axis_index(POSITIONS)

    packed = pack(attention_streams.transpose(1, 0, 2))
    long_start = jnp.sum(jnp.where(record_lengths == LONG, record_starts, 0))
    base, heads = lax.switch(
        lax.rem(long_start // (2 * rows), GROUP),
        [functools.partial(mixers, cut) for cut in range(GROUP)],
        packed,
        residual,
        hyena_streams.transpose(1, 0, 2),
        hyena_filter,
        record_starts,
    )
    scalars = jnp.stack([place, place, place]).astype(jnp.int32)

    with jax.named_scope("mean_square"):
        stream, squares = pl.pallas_call(
            stream_kernel,
            out_shape=(
                jax.ShapeDtypeStruct((rows, width), jnp.float32),
                jax.ShapeDtypeStruct((mp, 1, rows), jnp.float32),
            ),
            name="stream",
        )(base, heads)
        parts = lax.all_to_all(squares, "mp", 0, 0, tiled=True)
    with jax.named_scope("record_energy"):
        lines = [jnp.pad(x, (0, 128 - records))[None, :] for x in (record_starts, record_lengths)]
        mean, sums = pl.pallas_call(
            records_kernel,
            out_shape=(
                jax.ShapeDtypeStruct((rows, rows), jnp.float32),
                jax.ShapeDtypeStruct((seq, 1, 128), jnp.float32),
            ),
            in_specs=[SMEM, VMEM, VMEM, VMEM],
            name="records",
        )(scalars, *lines, parts)
        sums = lax.all_to_all(sums, POSITIONS, 0, 0, tiled=True)
        record_energy = jnp.sum(sums, axis=(0, 1))[:records] / record_lengths.astype(jnp.float32)
    mixed = pl.pallas_call(
        scale_kernel,
        out_shape=jax.ShapeDtypeStruct((rows, width), jnp.float32),
        cost_estimate=cost(1000),
        name="scale",
    )(stream, mean, norm_gain[None, :])
    return (mixed, record_energy)


def solution(mesh):
    fine = Mesh(mesh.devices.reshape(CHIPS, 2, mesh.shape["mp"]), ("z", "core", "mp"))
    return jax.shard_map(
        on_device,
        mesh=fine,
        in_specs=(
            P(POSITIONS, "mp"),
            P(POSITIONS, None, "mp"),
            P(None, "mp"),
            P(POSITIONS, None, "mp"),
            P("mp"),
            P(),
            P(),
            P(POSITIONS),
        ),
        out_specs=(P(POSITIONS, "mp"), P()),
        check_vma=False,
    )
```

```python
import functools

import jax
import jax.numpy as jnp
from jax import lax
from jax.experimental import pallas as pl
from jax.experimental.pallas import tpu as pltpu
from jax.sharding import Mesh
from jax.sharding import PartitionSpec as P

D = 8192
HEAD_DIM = 128
GROUP = 4
MASKED = -1e30
SCALE = HEAD_DIM**-0.5 * 1.4426950408889634
POSITIONS = ("z", "core")
CHIPS = 16
LONG = 2048
SMEM = pl.BlockSpec(memory_space=pltpu.SMEM)
VMEM = pl.BlockSpec(memory_space=pltpu.VMEM)


def cost(nanoseconds):
    return pl.CostEstimate(flops=nanoseconds * 1_000_000, bytes_accessed=1 << 20, transcendentals=0)


def pack_kernel(starts, lengths, x_ref, out_ref, cut_ref):
    for head in range(GROUP):
        for stream in range(3):
            out_ref[head, stream] = x_ref[stream, :, head * HEAD_DIM : (head + 1) * HEAD_DIM]
    long_start = jnp.int32(0)
    for record in range(starts.shape[0]):
        long_start = jnp.where(lengths[record] == LONG, starts[record], long_start)
    cut_ref[0] = lax.rem(long_start // (2 * x_ref.shape[1]) + 1, GROUP)


def pack(starts, lengths, streams):
    rows = streams.shape[1]
    return pl.pallas_call(
        pack_kernel,
        out_shape=(
            jax.ShapeDtypeStruct((GROUP, 3, rows, HEAD_DIM), streams.dtype),
            jax.ShapeDtypeStruct((1,), jnp.int32),
        ),
        in_specs=[SMEM, SMEM, VMEM],
        out_specs=(VMEM, SMEM),
        name="pack_heads",
    )(starts, lengths, streams)


def group_of(cut):
    return lax.rem(lax.axis_index("z") + CHIPS - cut, CHIPS) // GROUP


def attend_rows(q, query_pos, row_start, sources, state):
    rows = q.shape[0]
    scores = []
    for keys, _, first in sources:
        s = lax.dot_general(q, keys, (((1,), (1,)), ((), ())), preferred_element_type=jnp.float32)
        key_pos = jnp.concatenate(
            [here + lax.broadcasted_iota(jnp.int32, (1, rows), 1) for here in first], axis=1
        )
        allowed = (key_pos >= row_start) & (key_pos <= query_pos)
        scores.append(jnp.where(allowed, s * SCALE, MASKED))
    top = functools.reduce(jnp.maximum, [jnp.max(s, axis=1, keepdims=True) for s in scores])
    if state is not None:
        top = jnp.maximum(top, state[0])
    total = jnp.zeros((rows, 1), jnp.float32)
    summed = jnp.zeros((rows, HEAD_DIM), jnp.float32)
    for s, (_, values, _) in zip(scores, sources):
        weights = jnp.exp2(s - top)
        total = total + jnp.sum(weights, axis=1, keepdims=True)
        summed = summed + jnp.dot(
            weights.astype(jnp.bfloat16), values, preferred_element_type=jnp.float32
        )
    if state is not None:
        factor = jnp.exp2(state[0] - top)
        total = total + state[1] * factor
        summed = summed + state[2] * factor
    return top, total, summed


def chip_position(cut, group, place, core, rows):
    chip = lax.rem(group * GROUP + place + (cut + 2 * CHIPS), CHIPS)
    return (chip * 2 + core) * rows


def blocks_of(ref, low, high, offset=0):
    rows = ref.shape[2]
    return [ref[low:high, offset + i].reshape((high - low) * rows, HEAD_DIM) for i in range(2)]


def attend_kernel(cut, phase, starts, q_ref, *refs):
    group, core = group_of(cut), lax.axis_index("core")
    rows = q_ref.shape[2]
    place = lax.broadcasted_iota(jnp.int32, (rows, 1), 0)

    def source(ref, back, of_core, low, high, first=0, offset=0):
        blocks = blocks_of(ref, low, high, offset)
        where = range(first + low, first + high)
        return *blocks, [chip_position(cut, group - back, i, of_core, rows) for i in where]

    for block in range(GROUP):
        query_pos = chip_position(cut, group, block, core, rows) + place
        state = None
        if phase == 0:
            other, *outs = refs
            sources = [
                source(q_ref, 0, core, 0, block + 1, offset=1),
                source(other, 0, 1 - core, 0, block + 1),
            ]
        elif phase == 1:
            before, *state = refs[:4]
            outs = refs[4:]
            sources = [source(before, 1, core, 0, GROUP)]
        else:
            before, far, far_other, *state = refs[:6]
            outs = refs[6:]
            sources = [
                source(before, 1, 1 - core, 0, GROUP),
                source(far, 2, core, 0, 1, first=GROUP - 1),
                source(far_other, 2, 1 - core, 0, 1, first=GROUP - 1),
            ]
        top, total, summed = attend_rows(
            q_ref[block, 0],
            query_pos,
            row_starts(starts, query_pos),
            sources,
            state and [ref[block] for ref in state],
        )
        if phase < 2:
            outs[0][block], outs[1][block], outs[2][block] = top, total, summed
        else:
            outs[0][block] = summed / total


def attend(cut, phase, starts, received, *others):
    rows = received.shape[2]
    column = jax.ShapeDtypeStruct((GROUP, rows, 1), jnp.float32)
    full = jax.ShapeDtypeStruct((GROUP, rows, HEAD_DIM), jnp.float32)
    return pl.pallas_call(
        functools.partial(attend_kernel, cut, phase),
        out_shape=full if phase == 2 else (column, column, full),
        in_specs=[SMEM] + [VMEM] * (1 + len(others)),
        compiler_params=pltpu.CompilerParams(vmem_limit_bytes=32 * 1024 * 1024),
        cost_estimate=cost(2000),
        name=f"attend{phase}",
    )(starts, received, *others)


def row_starts(starts, positions):
    found = jnp.zeros_like(positions)
    for record in range(starts.shape[0]):
        here = starts[record]
        found = jnp.where(positions >= here, here, found)
    return found


def hyena_kernel(starts, residual, streams, rim, taps_ref, out_ref, padded):
    rows = residual.shape[0]
    edge = rim.shape[1]
    taps = taps_ref.shape[0]
    positions = lax.axis_index(POSITIONS) * rows + lax.broadcasted_iota(jnp.int32, (rows, 1), 0)
    first = row_starts(starts, positions)
    padded[:edge] = rim[0].astype(jnp.float32) * rim[1].astype(jnp.float32)
    padded[edge:] = streams[1].astype(jnp.float32) * streams[2].astype(jnp.float32)
    filtered = jnp.zeros(out_ref.shape, jnp.float32)
    for tap in range(taps):
        term = taps_ref[tap : tap + 1, :] * padded[edge - tap : edge - tap + rows]
        filtered = filtered + jnp.where(positions - tap >= first, term, 0.0)
    out_ref[...] = residual[...].astype(jnp.float32) + streams[0].astype(jnp.float32) * filtered


def stream_kernel(base, heads, stream_ref, squares_ref):
    rows = base.shape[0]
    squares = jnp.zeros((rows, HEAD_DIM), jnp.float32)
    for head in range(GROUP):
        columns = slice(head * HEAD_DIM, (head + 1) * HEAD_DIM)
        value = base[:, columns] + heads[head]
        stream_ref[:, columns] = value
        squares = squares + value * value
    line = jnp.sum(squares.T, axis=0, keepdims=True)
    for device in range(squares_ref.shape[0]):
        squares_ref[device] = line


def records_kernel(starts, lengths, parts, mean_ref, sums_ref):
    rows = parts.shape[2]
    line = jnp.sum(parts[:, 0, :], axis=0, keepdims=True) / D
    mean = jnp.broadcast_to(line, (rows, rows)).T
    mean_ref[...] = mean
    position = lax.axis_index(POSITIONS) * rows + lax.broadcasted_iota(jnp.int32, (rows, rows), 0)
    first = starts[...]
    inside = (position >= first) & (position < first + lengths[...])
    sums = jnp.sum(jnp.where(inside, mean, 0.0), axis=0, keepdims=True)
    for device in range(sums_ref.shape[0]):
        sums_ref[device] = sums


def scale_kernel(stream, mean, gain, out_ref):
    factor = lax.rsqrt(mean[...] + 1e-05)
    for head in range(GROUP):
        columns = slice(head * HEAD_DIM, (head + 1) * HEAD_DIM)
        out_ref[:, columns] = stream[:, columns] * factor * gain[:, columns]


def mixers(cut, packed, residual, streams, taps, starts):
    rows, width = residual.shape
    seq = lax.axis_size(POSITIONS)
    groups = [
        [(cut + GROUP * k + i) % CHIPS for i in range(GROUP)] for k in range(CHIPS // GROUP)
    ]
    swap = [(0, 1), (1, 0)]

    def along(value, chips, of_groups):
        pairs = [(i, (i + chips) % CHIPS) for k in of_groups for i in groups[k]]
        return lax.ppermute(value, "z", pairs)

    last = [3] if cut else []
    rim = lax.ppermute(streams[1:, rows - 16 :], POSITIONS, [(i, i + 1) for i in range(seq - 1)])
    received = lax.all_to_all(packed, "z", 0, 0, axis_index_groups=groups, tiled=True)
    far = along(received[GROUP - 1 :, 1:], 2 * GROUP, [0, 1] + last)
    key_value, rim = lax.optimization_barrier((received[:, 1:], rim))
    before = along(key_value, GROUP, [0, 1, 2] + last)
    other = lax.ppermute(key_value, "core", swap)
    base = pl.pallas_call(
        hyena_kernel,
        out_shape=jax.ShapeDtypeStruct((rows, width), jnp.float32),
        in_specs=[SMEM, VMEM, VMEM, VMEM, VMEM],
        out_specs=VMEM,
        scratch_shapes=[pltpu.VMEM((rows + 16, width), jnp.float32)],
        cost_estimate=cost(2000),
        name="hyena",
    )(starts, residual, streams, rim, taps)
    state = attend(cut, 0, starts, received, other)
    before, far, base, state = lax.optimization_barrier((before, far, base, state))
    before_other = lax.ppermute(before, "core", swap)
    far_other = lax.ppermute(far, "core", swap)
    state = attend(cut, 1, starts, received, before, *state)
    out = attend(cut, 2, starts, received, before_other, far, far_other, *state)
    heads = lax.all_to_all(out, "z", 0, 0, axis_index_groups=groups, tiled=True)
    return base, heads


def on_device(
    residual,
    hyena_streams,
    hyena_filter,
    attention_streams,
    norm_gain,
    record_starts,
    record_lengths,
    segment_ids,
):
    rows, width = residual.shape
    records = record_starts.shape[0]
    seq, mp = lax.axis_size(POSITIONS), lax.axis_size("mp")
    packed, cut = pack(record_starts, record_lengths, attention_streams.transpose(1, 0, 2))
    base, heads = lax.switch(
        cut[0],
        [functools.partial(mixers, here) for here in range(GROUP)],
        packed,
        residual,
        hyena_streams.transpose(1, 0, 2),
        hyena_filter,
        record_starts,
    )

    with jax.named_scope("mean_square"):
        stream, squares = pl.pallas_call(
            stream_kernel,
            out_shape=(
                jax.ShapeDtypeStruct((rows, width), jnp.float32),
                jax.ShapeDtypeStruct((mp, 1, rows), jnp.float32),
            ),
            name="stream",
        )(base, heads)
        parts = lax.all_to_all(squares, "mp", 0, 0, tiled=True)
    with jax.named_scope("record_energy"):
        lines = [jnp.pad(x, (0, 128 - records))[None, :] for x in (record_starts, record_lengths)]
        mean, sums = pl.pallas_call(
            records_kernel,
            out_shape=(
                jax.ShapeDtypeStruct((rows, rows), jnp.float32),
                jax.ShapeDtypeStruct((seq, 1, 128), jnp.float32),
            ),
            name="records",
        )(*lines, parts)
        sums = lax.all_to_all(sums, POSITIONS, 0, 0, tiled=True)
        record_energy = jnp.sum(sums, axis=(0, 1))[:records] / record_lengths.astype(jnp.float32)
    mixed = pl.pallas_call(
        scale_kernel,
        out_shape=jax.ShapeDtypeStruct((rows, width), jnp.float32),
        cost_estimate=cost(1000),
        name="scale",
    )(stream, mean, norm_gain[None, :])
    return (mixed, record_energy)


def solution(mesh):
    fine = Mesh(mesh.devices.reshape(CHIPS, 2, mesh.shape["mp"]), ("z", "core", "mp"))
    return jax.shard_map(
        on_device,
        mesh=fine,
        in_specs=(
            P(POSITIONS, "mp"),
            P(POSITIONS, None, "mp"),
            P(None, "mp"),
            P(POSITIONS, None, "mp"),
            P("mp"),
            P(),
            P(),
            P(POSITIONS),
        ),
        out_specs=(P(POSITIONS, "mp"), P()),
        check_vma=False,
    )
```

```python
import functools

import jax
import jax.numpy as jnp
from jax import lax
from jax.experimental import pallas as pl
from jax.experimental.pallas import tpu as pltpu
from jax.sharding import Mesh
from jax.sharding import PartitionSpec as P

D = 8192
HEAD_DIM = 128
GROUP = 4
MASKED = -1e30
SCALE = HEAD_DIM**-0.5 * 1.4426950408889634
POSITIONS = ("z", "core")
CHIPS = 16
LONG = 2048
SMEM = pl.BlockSpec(memory_space=pltpu.SMEM)
VMEM = pl.BlockSpec(memory_space=pltpu.VMEM)


def cost(nanoseconds):
    return pl.CostEstimate(flops=nanoseconds * 1_000_000, bytes_accessed=1 << 20, transcendentals=0)


def pack_kernel(starts, lengths, x_ref, out_ref, chip_ref):
    for head in range(GROUP):
        for stream in range(3):
            out_ref[head, stream] = x_ref[stream, :, head * HEAD_DIM : (head + 1) * HEAD_DIM]
    long_start = jnp.int32(0)
    for record in range(starts.shape[0]):
        long_start = jnp.where(lengths[record] == LONG, starts[record], long_start)
    chip_ref[0] = long_start // (2 * x_ref.shape[1])


def pack(starts, lengths, streams):
    rows = streams.shape[1]
    return pl.pallas_call(
        pack_kernel,
        out_shape=(
            jax.ShapeDtypeStruct((GROUP, 3, rows, HEAD_DIM), streams.dtype),
            jax.ShapeDtypeStruct((1,), jnp.int32),
        ),
        in_specs=[SMEM, SMEM, VMEM],
        out_specs=(VMEM, SMEM),
        name="pack_heads",
    )(starts, lengths, streams)


def cut_of(long_chip):
    return (long_chip + 1) % GROUP, (long_chip + 1) // GROUP % 2


def group_of(cut):
    return lax.rem(lax.axis_index("z") + CHIPS - cut, CHIPS) // GROUP


def attend_rows(q, query_pos, row_start, sources, state):
    rows = q.shape[0]
    scores = []
    for keys, _, first in sources:
        s = lax.dot_general(q, keys, (((1,), (1,)), ((), ())), preferred_element_type=jnp.float32)
        key_pos = jnp.concatenate(
            [here + lax.broadcasted_iota(jnp.int32, (1, rows), 1) for here in first], axis=1
        )
        allowed = (key_pos >= row_start) & (key_pos <= query_pos)
        scores.append(jnp.where(allowed, s * SCALE, MASKED))
    top = functools.reduce(jnp.maximum, [jnp.max(s, axis=1, keepdims=True) for s in scores])
    if state is not None:
        top = jnp.maximum(top, state[0])
    total = jnp.zeros((rows, 1), jnp.float32)
    summed = jnp.zeros((rows, HEAD_DIM), jnp.float32)
    for s, (_, values, _) in zip(scores, sources):
        weights = jnp.exp2(s - top)
        total = total + jnp.sum(weights, axis=1, keepdims=True)
        summed = summed + jnp.dot(
            weights.astype(jnp.bfloat16), values, preferred_element_type=jnp.float32
        )
    if state is not None:
        factor = jnp.exp2(state[0] - top)
        total = total + state[1] * factor
        summed = summed + state[2] * factor
    return top, total, summed


def chip_position(cut, group, place, core, rows):
    chip = lax.rem(group * GROUP + place + (cut + 2 * CHIPS), CHIPS)
    return (chip * 2 + core) * rows


def blocks_of(ref, low, high, offset=0):
    rows = ref.shape[2]
    return [ref[low:high, offset + i].reshape((high - low) * rows, HEAD_DIM) for i in range(2)]


def attend_kernel(long_chip, phase, starts, q_ref, *refs):
    cut, even = cut_of(long_chip)
    group, core = group_of(cut), lax.axis_index("core")
    rows = q_ref.shape[2]
    place = lax.broadcasted_iota(jnp.int32, (rows, 1), 0)

    is_even = lax.rem(group + even, 2) == 0

    def own(ref, of_core, count, offset=0):
        blocks = blocks_of(ref, 0, count, offset)
        return *blocks, [chip_position(cut, group, i, of_core, rows) for i in range(count)]

    def before(ref, of_core):
        first = [chip_position(cut, group - 1, i, of_core, rows) for i in range(GROUP)]
        return *blocks_of(ref, 0, GROUP), [jnp.where(is_even, -2 * LONG, here) for here in first]

    def edge(ref, of_core):
        back = jnp.where(is_even, 1, 2)
        return ref[0, 0], ref[0, 1], [chip_position(cut, group - back, GROUP - 1, of_core, rows)]

    for block in range(GROUP):
        query_pos = chip_position(cut, group, block, core, rows) + place
        state = None
        if phase == 0:
            other, *outs = refs
            sources = [own(q_ref, core, block + 1, 1), own(other, 1 - core, block + 1)]
        else:
            from_core = core if phase == 1 else 1 - core
            sources = [before(refs[0], from_core), edge(refs[1], from_core)]
            state, outs = refs[2:5], refs[5:]
        top, total, summed = attend_rows(
            q_ref[block, 0],
            query_pos,
            row_starts(starts, query_pos),
            sources,
            state and [ref[block] for ref in state],
        )
        if phase < 2:
            outs[0][block], outs[1][block], outs[2][block] = top, total, summed
        else:
            outs[0][block] = summed / total


def attend(long_chip, phase, starts, received, *others):
    rows = received.shape[2]
    column = jax.ShapeDtypeStruct((GROUP, rows, 1), jnp.float32)
    full = jax.ShapeDtypeStruct((GROUP, rows, HEAD_DIM), jnp.float32)
    return pl.pallas_call(
        functools.partial(attend_kernel, long_chip, phase),
        out_shape=full if phase == 2 else (column, column, full),
        in_specs=[SMEM] + [VMEM] * (1 + len(others)),
        compiler_params=pltpu.CompilerParams(vmem_limit_bytes=32 * 1024 * 1024),
        cost_estimate=cost(2000),
        name=f"attend{phase}",
    )(starts, received, *others)


def row_starts(starts, positions):
    found = jnp.zeros_like(positions)
    for record in range(starts.shape[0]):
        here = starts[record]
        found = jnp.where(positions >= here, here, found)
    return found


def hyena_kernel(starts, residual, streams, rim, taps_ref, out_ref, padded):
    rows = residual.shape[0]
    edge = rim.shape[1]
    taps = taps_ref.shape[0]
    positions = lax.axis_index(POSITIONS) * rows + lax.broadcasted_iota(jnp.int32, (rows, 1), 0)
    first = row_starts(starts, positions)
    padded[:edge] = rim[0].astype(jnp.float32) * rim[1].astype(jnp.float32)
    padded[edge:] = streams[1].astype(jnp.float32) * streams[2].astype(jnp.float32)
    filtered = jnp.zeros(out_ref.shape, jnp.float32)
    for tap in range(taps):
        term = taps_ref[tap : tap + 1, :] * padded[edge - tap : edge - tap + rows]
        filtered = filtered + jnp.where(positions - tap >= first, term, 0.0)
    out_ref[...] = residual[...].astype(jnp.float32) + streams[0].astype(jnp.float32) * filtered


def stream_kernel(base, heads, stream_ref, squares_ref):
    rows = base.shape[0]
    squares = jnp.zeros((rows, HEAD_DIM), jnp.float32)
    for head in range(GROUP):
        columns = slice(head * HEAD_DIM, (head + 1) * HEAD_DIM)
        value = base[:, columns] + heads[head]
        stream_ref[:, columns] = value
        squares = squares + value * value
    line = jnp.sum(squares.T, axis=0, keepdims=True)
    for device in range(squares_ref.shape[0]):
        squares_ref[device] = line


def records_kernel(starts, lengths, parts, mean_ref, sums_ref):
    rows = parts.shape[2]
    line = jnp.sum(parts[:, 0, :], axis=0, keepdims=True) / D
    mean = jnp.broadcast_to(line, (rows, rows)).T
    mean_ref[...] = mean
    position = lax.axis_index(POSITIONS) * rows + lax.broadcasted_iota(jnp.int32, (rows, rows), 0)
    first = starts[...]
    inside = (position >= first) & (position < first + lengths[...])
    sums = jnp.sum(jnp.where(inside, mean, 0.0), axis=0, keepdims=True)
    for device in range(sums_ref.shape[0]):
        sums_ref[device] = sums


def scale_kernel(stream, mean, gain, out_ref):
    factor = lax.rsqrt(mean[...] + 1e-05)
    for head in range(GROUP):
        columns = slice(head * HEAD_DIM, (head + 1) * HEAD_DIM)
        out_ref[:, columns] = stream[:, columns] * factor * gain[:, columns]


def mixers(long_chip, packed, residual, streams, taps, starts):
    rows, width = residual.shape
    cut, even = cut_of(long_chip)
    seq = lax.axis_size(POSITIONS)
    groups = [
        [(cut + GROUP * k + i) % CHIPS for i in range(GROUP)] for k in range(CHIPS // GROUP)
    ]
    swap = [(0, 1), (1, 0)]

    def along(value, count, of_groups):
        pairs = [(i, (i + count * GROUP) % CHIPS) for k in of_groups for i in groups[k]]
        return lax.ppermute(value, "z", pairs)

    evens, odds = [even, even + 2], [1 - even, 3 - even]
    rim = lax.ppermute(streams[1:, rows - 16 :], POSITIONS, [(i, i + 1) for i in range(seq - 1)])
    received = lax.all_to_all(packed, "z", 0, 0, axis_index_groups=groups, tiled=True)
    key_value, rim = lax.optimization_barrier((received[:, 1:], rim))
    before = along(key_value, 1, evens)
    last = received[GROUP - 1 :, 1:]
    edge = along(last, 2, odds) + along(last, 1, odds)
    base = pl.pallas_call(
        hyena_kernel,
        out_shape=jax.ShapeDtypeStruct((rows, width), jnp.float32),
        in_specs=[SMEM, VMEM, VMEM, VMEM, VMEM],
        out_specs=VMEM,
        scratch_shapes=[pltpu.VMEM((rows + 16, width), jnp.float32)],
        cost_estimate=cost(2000),
        name="hyena",
    )(starts, residual, streams, rim, taps)
    key_value, base = lax.optimization_barrier((key_value, base))
    other = lax.ppermute(key_value, "core", swap)
    state = attend(long_chip, 0, starts, received, other)
    edge_other = lax.ppermute(edge, "core", swap)
    before, edge, edge_other, state = lax.optimization_barrier((before, edge, edge_other, state))
    before_other = lax.ppermute(before, "core", swap)
    state = attend(long_chip, 1, starts, received, before, edge, *state)
    out = attend(long_chip, 2, starts, received, before_other, edge_other, *state)
    heads = lax.all_to_all(out, "z", 0, 0, axis_index_groups=groups, tiled=True)
    return base, heads


def on_device(
    residual,
    hyena_streams,
    hyena_filter,
    attention_streams,
    norm_gain,
    record_starts,
    record_lengths,
    segment_ids,
):
    rows, width = residual.shape
    records = record_starts.shape[0]
    seq, mp = lax.axis_size(POSITIONS), lax.axis_size("mp")
    packed, chip = pack(record_starts, record_lengths, attention_streams.transpose(1, 0, 2))
    base, heads = lax.switch(
        chip[0],
        [functools.partial(mixers, here) for here in range(CHIPS - LONG // (2 * rows) + 1)],
        packed,
        residual,
        hyena_streams.transpose(1, 0, 2),
        hyena_filter,
        record_starts,
    )

    with jax.named_scope("mean_square"):
        stream, squares = pl.pallas_call(
            stream_kernel,
            out_shape=(
                jax.ShapeDtypeStruct((rows, width), jnp.float32),
                jax.ShapeDtypeStruct((mp, 1, rows), jnp.float32),
            ),
            name="stream",
        )(base, heads)
        parts = lax.all_to_all(squares, "mp", 0, 0, tiled=True)
    with jax.named_scope("record_energy"):
        lines = [jnp.pad(x, (0, 128 - records))[None, :] for x in (record_starts, record_lengths)]
        mean, sums = pl.pallas_call(
            records_kernel,
            out_shape=(
                jax.ShapeDtypeStruct((rows, rows), jnp.float32),
                jax.ShapeDtypeStruct((seq, 1, 128), jnp.float32),
            ),
            name="records",
        )(*lines, parts)
        sums = lax.all_to_all(sums, POSITIONS, 0, 0, tiled=True)
        record_energy = jnp.sum(sums, axis=(0, 1))[:records] / record_lengths.astype(jnp.float32)
    mixed = pl.pallas_call(
        scale_kernel,
        out_shape=jax.ShapeDtypeStruct((rows, width), jnp.float32),
        cost_estimate=cost(1000),
        name="scale",
    )(stream, mean, norm_gain[None, :])
    return (mixed, record_energy)


def solution(mesh):
    fine = Mesh(mesh.devices.reshape(CHIPS, 2, mesh.shape["mp"]), ("z", "core", "mp"))
    return jax.shard_map(
        on_device,
        mesh=fine,
        in_specs=(
            P(POSITIONS, "mp"),
            P(POSITIONS, None, "mp"),
            P(None, "mp"),
            P(POSITIONS, None, "mp"),
            P("mp"),
            P(),
            P(),
            P(POSITIONS),
        ),
        out_specs=(P(POSITIONS, "mp"), P()),
        check_vma=False,
    )
```

```python
import functools

import jax
import jax.numpy as jnp
from jax import lax
from jax.experimental import pallas as pl
from jax.experimental.pallas import tpu as pltpu
from jax.sharding import Mesh
from jax.sharding import PartitionSpec as P

D = 8192
HEAD_DIM = 128
GROUP = 4
MASKED = -1e30
SCALE = HEAD_DIM**-0.5 * 1.4426950408889634
POSITIONS = ("z", "core")
CHIPS = 16
LONG = 2048
SMEM = pl.BlockSpec(memory_space=pltpu.SMEM)
VMEM = pl.BlockSpec(memory_space=pltpu.VMEM)


def cost(nanoseconds):
    return pl.CostEstimate(flops=nanoseconds * 1_000_000, bytes_accessed=1 << 20, transcendentals=0)


def as_line(scalars):
    lane = lax.broadcasted_iota(jnp.int32, (1, HEAD_DIM), 1)
    line = jnp.zeros((1, HEAD_DIM), jnp.int32)
    for record in range(scalars.shape[0]):
        line = jnp.where(lane == record, scalars[record], line)
    return line


def pack_kernel(starts, lengths, x_ref, out_ref, lines_ref, chip_ref):
    for head in range(GROUP):
        for stream in range(3):
            out_ref[head, stream] = x_ref[stream, :, head * HEAD_DIM : (head + 1) * HEAD_DIM]
    long_start = jnp.int32(0)
    for record in range(starts.shape[0]):
        long_start = jnp.where(lengths[record] == LONG, starts[record], long_start)
    chip_ref[0] = long_start // (2 * x_ref.shape[1])
    lines_ref[0] = as_line(starts)
    lines_ref[1] = as_line(lengths)


def pack(starts, lengths, streams):
    rows = streams.shape[1]
    return pl.pallas_call(
        pack_kernel,
        out_shape=(
            jax.ShapeDtypeStruct((GROUP, 3, rows, HEAD_DIM), streams.dtype),
            jax.ShapeDtypeStruct((2, 1, HEAD_DIM), jnp.int32),
            jax.ShapeDtypeStruct((1,), jnp.int32),
        ),
        in_specs=[SMEM, SMEM, VMEM],
        out_specs=(VMEM, VMEM, SMEM),
        name="pack_heads",
    )(starts, lengths, streams)


def cut_of(long_chip):
    return (long_chip + 1) % GROUP, (long_chip + 1) // GROUP % 2


def group_of(cut):
    return lax.rem(lax.axis_index("z") + CHIPS - cut, CHIPS) // GROUP


def attend_rows(q, query_pos, row_start, sources, state):
    rows = q.shape[0]
    scores = []
    for keys, _, first in sources:
        s = lax.dot_general(q, keys, (((1,), (1,)), ((), ())), preferred_element_type=jnp.float32)
        key_pos = jnp.concatenate(
            [here + lax.broadcasted_iota(jnp.int32, (1, rows), 1) for here in first], axis=1
        )
        allowed = (key_pos >= row_start) & (key_pos <= query_pos)
        scores.append(jnp.where(allowed, s * SCALE, MASKED))
    top = functools.reduce(jnp.maximum, [jnp.max(s, axis=1, keepdims=True) for s in scores])
    if state is not None:
        top = jnp.maximum(top, state[0])
    total = jnp.zeros((rows, 1), jnp.float32)
    summed = jnp.zeros((rows, HEAD_DIM), jnp.float32)
    for s, (_, values, _) in zip(scores, sources):
        weights = jnp.exp2(s - top)
        total = total + jnp.sum(weights, axis=1, keepdims=True)
        summed = summed + jnp.dot(
            weights.astype(jnp.bfloat16), values, preferred_element_type=jnp.float32
        )
    if state is not None:
        factor = jnp.exp2(state[0] - top)
        total = total + state[1] * factor
        summed = summed + state[2] * factor
    return top, total, summed


def chip_position(cut, group, place, core, rows):
    chip = lax.rem(group * GROUP + place + (cut + 2 * CHIPS), CHIPS)
    return (chip * 2 + core) * rows


def blocks_of(ref, low, high, offset=0):
    rows = ref.shape[2]
    return [ref[low:high, offset + i].reshape((high - low) * rows, HEAD_DIM) for i in range(2)]


def attend_kernel(long_chip, phase, starts, q_ref, *refs):
    cut, even = cut_of(long_chip)
    group, core = group_of(cut), lax.axis_index("core")
    rows = q_ref.shape[2]
    place = lax.broadcasted_iota(jnp.int32, (rows, 1), 0)

    is_even = lax.rem(group + even, 2) == 0

    def own(ref, of_core, count, offset=0):
        blocks = blocks_of(ref, 0, count, offset)
        return *blocks, [chip_position(cut, group, i, of_core, rows) for i in range(count)]

    def before(ref, of_core):
        first = [chip_position(cut, group - 1, i, of_core, rows) for i in range(GROUP)]
        return *blocks_of(ref, 0, GROUP), [jnp.where(is_even, -2 * LONG, here) for here in first]

    def edge(ref, of_core):
        back = jnp.where(is_even, 1, 2)
        return ref[0, 0], ref[0, 1], [chip_position(cut, group - back, GROUP - 1, of_core, rows)]

    for block in range(GROUP):
        query_pos = chip_position(cut, group, block, core, rows) + place
        state = None
        if phase == 0:
            other, *outs = refs
            sources = [own(q_ref, core, block + 1, 1), own(other, 1 - core, block + 1)]
        else:
            from_core = core if phase == 1 else 1 - core
            sources = [before(refs[0], from_core), edge(refs[1], from_core)]
            state, outs = refs[2:5], refs[5:]
        top, total, summed = attend_rows(
            q_ref[block, 0],
            query_pos,
            row_starts(starts, query_pos),
            sources,
            state and [ref[block] for ref in state],
        )
        if phase < 2:
            outs[0][block], outs[1][block], outs[2][block] = top, total, summed
        else:
            outs[0][block] = summed / total


def attend(long_chip, phase, starts, received, *others):
    rows = received.shape[2]
    column = jax.ShapeDtypeStruct((GROUP, rows, 1), jnp.float32)
    full = jax.ShapeDtypeStruct((GROUP, rows, HEAD_DIM), jnp.float32)
    return pl.pallas_call(
        functools.partial(attend_kernel, long_chip, phase),
        out_shape=full if phase == 2 else (column, column, full),
        in_specs=[SMEM] + [VMEM] * (1 + len(others)),
        compiler_params=pltpu.CompilerParams(vmem_limit_bytes=32 * 1024 * 1024),
        cost_estimate=cost(2000),
        name=f"attend{phase}",
    )(starts, received, *others)


def row_starts(starts, positions):
    found = jnp.zeros_like(positions)
    for record in range(starts.shape[0]):
        here = starts[record]
        found = jnp.where(positions >= here, here, found)
    return found


def hyena_kernel(starts, residual, streams, rim, taps_ref, out_ref, padded):
    rows = residual.shape[0]
    edge = rim.shape[1]
    taps = taps_ref.shape[0]
    positions = lax.axis_index(POSITIONS) * rows + lax.broadcasted_iota(jnp.int32, (rows, 1), 0)
    first = row_starts(starts, positions)
    padded[:edge] = rim[0].astype(jnp.float32) * rim[1].astype(jnp.float32)
    padded[edge:] = streams[1].astype(jnp.float32) * streams[2].astype(jnp.float32)
    filtered = jnp.zeros(out_ref.shape, jnp.float32)
    for tap in range(taps):
        term = taps_ref[tap : tap + 1, :] * padded[edge - tap : edge - tap + rows]
        filtered = filtered + jnp.where(positions - tap >= first, term, 0.0)
    out_ref[...] = residual[...].astype(jnp.float32) + streams[0].astype(jnp.float32) * filtered


def stream_kernel(base, heads, stream_ref, squares_ref):
    rows = base.shape[0]
    squares = jnp.zeros((rows, HEAD_DIM), jnp.float32)
    for head in range(GROUP):
        columns = slice(head * HEAD_DIM, (head + 1) * HEAD_DIM)
        value = base[:, columns] + heads[head]
        stream_ref[:, columns] = value
        squares = squares + value * value
    line = jnp.sum(squares.T, axis=0, keepdims=True)
    for device in range(squares_ref.shape[0]):
        squares_ref[device] = line


def records_kernel(lines, parts, mean_ref, sums_ref):
    rows = parts.shape[2]
    line = jnp.sum(parts[:, 0, :], axis=0, keepdims=True) / D
    mean = jnp.broadcast_to(line, (rows, rows)).T
    mean_ref[...] = mean
    position = lax.axis_index(POSITIONS) * rows + lax.broadcasted_iota(jnp.int32, (rows, rows), 0)
    first = lines[0]
    inside = (position >= first) & (position < first + lines[1])
    sums = jnp.sum(jnp.where(inside, mean, 0.0), axis=0, keepdims=True)
    for device in range(sums_ref.shape[0]):
        sums_ref[device] = sums


def scale_kernel(stream, mean, gain, out_ref):
    factor = lax.rsqrt(mean[...] + 1e-05)
    for head in range(GROUP):
        columns = slice(head * HEAD_DIM, (head + 1) * HEAD_DIM)
        out_ref[:, columns] = stream[:, columns] * factor * gain[:, columns]


def mixers(long_chip, packed, residual, streams, taps, starts):
    rows, width = residual.shape
    cut, even = cut_of(long_chip)
    seq = lax.axis_size(POSITIONS)
    groups = [
        [(cut + GROUP * k + i) % CHIPS for i in range(GROUP)] for k in range(CHIPS // GROUP)
    ]
    swap = [(0, 1), (1, 0)]

    def along(value, count, of_groups):
        pairs = [(i, (i + count * GROUP) % CHIPS) for k in of_groups for i in groups[k]]
        return lax.ppermute(value, "z", pairs)

    evens, odds = [even, even + 2], [1 - even, 3 - even]
    rim = lax.ppermute(streams[1:, rows - 16 :], POSITIONS, [(i, i + 1) for i in range(seq - 1)])
    received = lax.all_to_all(packed, "z", 0, 0, axis_index_groups=groups, tiled=True)
    key_value, rim = lax.optimization_barrier((received[:, 1:], rim))
    before = along(key_value, 1, evens)
    last = received[GROUP - 1 :, 1:]
    edge = along(last, 2, odds) + along(last, 1, odds)
    base = pl.pallas_call(
        hyena_kernel,
        out_shape=jax.ShapeDtypeStruct((rows, width), jnp.float32),
        in_specs=[SMEM, VMEM, VMEM, VMEM, VMEM],
        out_specs=VMEM,
        scratch_shapes=[pltpu.VMEM((rows + 16, width), jnp.float32)],
        cost_estimate=cost(2000),
        name="hyena",
    )(starts, residual, streams, rim, taps)
    key_value, base = lax.optimization_barrier((key_value, base))
    other = lax.ppermute(key_value, "core", swap)
    state = attend(long_chip, 0, starts, received, other)
    edge_other = lax.ppermute(edge, "core", swap)
    before, edge, edge_other, state = lax.optimization_barrier((before, edge, edge_other, state))
    before_other = lax.ppermute(before, "core", swap)
    state = attend(long_chip, 1, starts, received, before, edge, *state)
    out = attend(long_chip, 2, starts, received, before_other, edge_other, *state)
    out = out.astype(jnp.float16)
    heads = lax.all_to_all(out, "z", 0, 0, axis_index_groups=groups, tiled=True)
    return base, heads.astype(jnp.float32)


def on_device(
    residual,
    hyena_streams,
    hyena_filter,
    attention_streams,
    norm_gain,
    record_starts,
    record_lengths,
    segment_ids,
):
    rows, width = residual.shape
    records = record_starts.shape[0]
    seq, mp = lax.axis_size(POSITIONS), lax.axis_size("mp")
    packed, lines, chip = pack(record_starts, record_lengths, attention_streams.transpose(1, 0, 2))
    base, heads = lax.switch(
        chip[0],
        [functools.partial(mixers, here) for here in range(CHIPS - LONG // (2 * rows) + 1)],
        packed,
        residual,
        hyena_streams.transpose(1, 0, 2),
        hyena_filter,
        record_starts,
    )

    with jax.named_scope("mean_square"):
        stream, squares = pl.pallas_call(
            stream_kernel,
            out_shape=(
                jax.ShapeDtypeStruct((rows, width), jnp.float32),
                jax.ShapeDtypeStruct((mp, 1, rows), jnp.float32),
            ),
            name="stream",
        )(base, heads)
        parts = lax.all_to_all(squares, "mp", 0, 0, tiled=True)
    with jax.named_scope("record_energy"):
        mean, sums = pl.pallas_call(
            records_kernel,
            out_shape=(
                jax.ShapeDtypeStruct((rows, rows), jnp.float32),
                jax.ShapeDtypeStruct((seq, 1, 128), jnp.float32),
            ),
            name="records",
        )(lines, parts)
        sums = lax.all_to_all(sums, POSITIONS, 0, 0, tiled=True)
        record_energy = jnp.sum(sums, axis=(0, 1))[:records] / record_lengths.astype(jnp.float32)
    mixed = pl.pallas_call(
        scale_kernel,
        out_shape=jax.ShapeDtypeStruct((rows, width), jnp.float32),
        cost_estimate=cost(1000),
        name="scale",
    )(stream, mean, norm_gain[None, :])
    return (mixed, record_energy)


def solution(mesh):
    fine = Mesh(mesh.devices.reshape(CHIPS, 2, mesh.shape["mp"]), ("z", "core", "mp"))
    return jax.shard_map(
        on_device,
        mesh=fine,
        in_specs=(
            P(POSITIONS, "mp"),
            P(POSITIONS, None, "mp"),
            P(None, "mp"),
            P(POSITIONS, None, "mp"),
            P("mp"),
            P(),
            P(),
            P(POSITIONS),
        ),
        out_specs=(P(POSITIONS, "mp"), P()),
        check_vma=False,
    )
```

```python
import functools

import jax
import jax.numpy as jnp
from jax import lax
from jax.experimental import pallas as pl
from jax.experimental.pallas import tpu as pltpu
from jax.sharding import Mesh
from jax.sharding import PartitionSpec as P

D = 8192
HEAD_DIM = 128
GROUP = 4
MASKED = -1e30
SCALE = HEAD_DIM**-0.5 * 1.4426950408889634
POSITIONS = ("z", "core")
CHIPS = 16
LONG = 2048
SMEM = pl.BlockSpec(memory_space=pltpu.SMEM)
VMEM = pl.BlockSpec(memory_space=pltpu.VMEM)


def cost(nanoseconds):
    return pl.CostEstimate(flops=nanoseconds * 1_000_000, bytes_accessed=1 << 20, transcendentals=0)


def as_line(scalars):
    lane = lax.broadcasted_iota(jnp.int32, (1, HEAD_DIM), 1)
    line = jnp.zeros((1, HEAD_DIM), jnp.int32)
    for record in range(scalars.shape[0]):
        line = jnp.where(lane == record, scalars[record], line)
    return line


def pack_kernel(starts, lengths, x_ref, out_ref, lines_ref, chip_ref):
    for head in range(GROUP):
        for stream in range(3):
            out_ref[head, stream] = x_ref[stream, :, head * HEAD_DIM : (head + 1) * HEAD_DIM]
    long_start = jnp.int32(0)
    for record in range(starts.shape[0]):
        long_start = jnp.where(lengths[record] == LONG, starts[record], long_start)
    chip_ref[0] = long_start // (2 * x_ref.shape[1])
    lines_ref[0] = as_line(starts)
    lines_ref[1] = as_line(lengths)


def pack(starts, lengths, streams):
    rows = streams.shape[1]
    return pl.pallas_call(
        pack_kernel,
        out_shape=(
            jax.ShapeDtypeStruct((GROUP, 3, rows, HEAD_DIM), streams.dtype),
            jax.ShapeDtypeStruct((2, 1, HEAD_DIM), jnp.int32),
            jax.ShapeDtypeStruct((1,), jnp.int32),
        ),
        in_specs=[SMEM, SMEM, VMEM],
        out_specs=(VMEM, VMEM, SMEM),
        name="pack_heads",
    )(starts, lengths, streams)


def cut_of(long_chip):
    return (long_chip + 1) % GROUP, (long_chip + 1) // GROUP % 2


def group_of(cut):
    return lax.rem(lax.axis_index("z") + CHIPS - cut, CHIPS) // GROUP


def attend_rows(q, query_pos, row_start, sources, state):
    rows = q.shape[0]
    scores = []
    for keys, _, first in sources:
        s = lax.dot_general(q, keys, (((1,), (1,)), ((), ())), preferred_element_type=jnp.float32)
        key_pos = jnp.concatenate(
            [here + lax.broadcasted_iota(jnp.int32, (1, rows), 1) for here in first], axis=1
        )
        allowed = (key_pos >= row_start) & (key_pos <= query_pos)
        scores.append(jnp.where(allowed, s * SCALE, MASKED))
    top = functools.reduce(jnp.maximum, [jnp.max(s, axis=1, keepdims=True) for s in scores])
    if state is not None:
        top = jnp.maximum(top, state[0])
    total = jnp.zeros((rows, 1), jnp.float32)
    summed = jnp.zeros((rows, HEAD_DIM), jnp.float32)
    for s, (_, values, _) in zip(scores, sources):
        weights = jnp.exp2(s - top)
        total = total + jnp.sum(weights, axis=1, keepdims=True)
        summed = summed + jnp.dot(
            weights.astype(jnp.bfloat16), values, preferred_element_type=jnp.float32
        )
    if state is not None:
        factor = jnp.exp2(state[0] - top)
        total = total + state[1] * factor
        summed = summed + state[2] * factor
    return top, total, summed


def chip_position(cut, group, place, core, rows):
    chip = lax.rem(group * GROUP + place + (cut + 2 * CHIPS), CHIPS)
    return (chip * 2 + core) * rows


def blocks_of(ref, low, high, offset=0):
    rows = ref.shape[2]
    return [ref[low:high, offset + i].reshape((high - low) * rows, HEAD_DIM) for i in range(2)]


def attend_kernel(long_chip, phase, starts, q_ref, *refs):
    cut, even = cut_of(long_chip)
    group, core = group_of(cut), lax.axis_index("core")
    rows = q_ref.shape[2]
    place = lax.broadcasted_iota(jnp.int32, (rows, 1), 0)

    is_even = lax.rem(group + even, 2) == 0

    def own(ref, of_core, count, offset=0):
        blocks = blocks_of(ref, 0, count, offset)
        return *blocks, [chip_position(cut, group, i, of_core, rows) for i in range(count)]

    def before(ref, of_core):
        first = [chip_position(cut, group - 1, i, of_core, rows) for i in range(GROUP)]
        return *blocks_of(ref, 0, GROUP), [jnp.where(is_even, -2 * LONG, here) for here in first]

    def edge(ref, of_core):
        back = jnp.where(is_even, 1, 2)
        return ref[0, 0], ref[0, 1], [chip_position(cut, group - back, GROUP - 1, of_core, rows)]

    if phase == 0:
        other, *outs = refs
        sources = [own(q_ref, core, GROUP, 1), own(other, 1 - core, GROUP)]
    else:
        from_core = core if phase == 1 else 1 - core
        sources = [before(refs[0], from_core), edge(refs[1], from_core)]
        state, outs = refs[2:5], refs[5:]

    @pl.loop(0, GROUP)
    def _(block):
        query_pos = chip_position(cut, group, block, core, rows) + place
        top, total, summed = attend_rows(
            q_ref[block, 0],
            query_pos,
            row_starts(starts, query_pos),
            sources,
            None if phase == 0 else [ref[block] for ref in state],
        )
        if phase < 2:
            outs[0][block], outs[1][block], outs[2][block] = top, total, summed
        else:
            outs[0][block] = summed / total


def attend(long_chip, phase, starts, received, *others):
    rows = received.shape[2]
    column = jax.ShapeDtypeStruct((GROUP, rows, 1), jnp.float32)
    full = jax.ShapeDtypeStruct((GROUP, rows, HEAD_DIM), jnp.float32)
    return pl.pallas_call(
        functools.partial(attend_kernel, long_chip, phase),
        out_shape=full if phase == 2 else (column, column, full),
        in_specs=[SMEM] + [VMEM] * (1 + len(others)),
        compiler_params=pltpu.CompilerParams(vmem_limit_bytes=32 * 1024 * 1024),
        cost_estimate=cost(2000),
        name=f"attend{phase}",
    )(starts, received, *others)


def row_starts(starts, positions):
    found = jnp.zeros_like(positions)
    for record in range(starts.shape[0]):
        here = starts[record]
        found = jnp.where(positions >= here, here, found)
    return found


def hyena_kernel(starts, residual, streams, rim, taps_ref, out_ref, padded):
    rows = residual.shape[0]
    edge = rim.shape[1]
    taps = taps_ref.shape[0]
    positions = lax.axis_index(POSITIONS) * rows + lax.broadcasted_iota(jnp.int32, (rows, 1), 0)
    first = row_starts(starts, positions)
    padded[:edge] = rim[0].astype(jnp.float32) * rim[1].astype(jnp.float32)
    padded[edge:] = streams[1].astype(jnp.float32) * streams[2].astype(jnp.float32)
    filtered = jnp.zeros(out_ref.shape, jnp.float32)
    for tap in range(taps):
        term = taps_ref[tap : tap + 1, :] * padded[edge - tap : edge - tap + rows]
        filtered = filtered + jnp.where(positions - tap >= first, term, 0.0)
    out_ref[...] = residual[...].astype(jnp.float32) + streams[0].astype(jnp.float32) * filtered


def stream_kernel(base, heads, stream_ref, squares_ref):
    rows = base.shape[0]
    squares = jnp.zeros((rows, HEAD_DIM), jnp.float32)
    for head in range(GROUP):
        columns = slice(head * HEAD_DIM, (head + 1) * HEAD_DIM)
        value = base[:, columns] + heads[head]
        stream_ref[:, columns] = value
        squares = squares + value * value
    line = jnp.sum(squares.T, axis=0, keepdims=True)
    for device in range(squares_ref.shape[0]):
        squares_ref[device] = line


def records_kernel(lines, parts, mean_ref, sums_ref):
    rows = parts.shape[2]
    line = jnp.sum(parts[:, 0, :], axis=0, keepdims=True) / D
    mean = jnp.broadcast_to(line, (rows, rows)).T
    mean_ref[...] = mean
    position = lax.axis_index(POSITIONS) * rows + lax.broadcasted_iota(jnp.int32, (rows, rows), 0)
    first = lines[0]
    inside = (position >= first) & (position < first + lines[1])
    sums = jnp.sum(jnp.where(inside, mean, 0.0), axis=0, keepdims=True)
    for device in range(sums_ref.shape[0]):
        sums_ref[device] = sums


def scale_kernel(stream, mean, gain, out_ref):
    factor = lax.rsqrt(mean[...] + 1e-05)
    for head in range(GROUP):
        columns = slice(head * HEAD_DIM, (head + 1) * HEAD_DIM)
        out_ref[:, columns] = stream[:, columns] * factor * gain[:, columns]


def mixers(long_chip, packed, residual, streams, taps, starts):
    rows, width = residual.shape
    cut, even = cut_of(long_chip)
    seq = lax.axis_size(POSITIONS)
    groups = [
        [(cut + GROUP * k + i) % CHIPS for i in range(GROUP)] for k in range(CHIPS // GROUP)
    ]
    swap = [(0, 1), (1, 0)]

    def along(value, count, of_groups):
        pairs = [(i, (i + count * GROUP) % CHIPS) for k in of_groups for i in groups[k]]
        return lax.ppermute(value, "z", pairs)

    evens, odds = [even, even + 2], [1 - even, 3 - even]
    rim = lax.ppermute(streams[1:, rows - 16 :], POSITIONS, [(i, i + 1) for i in range(seq - 1)])
    received = lax.all_to_all(packed, "z", 0, 0, axis_index_groups=groups, tiled=True)
    key_value, rim = lax.optimization_barrier((received[:, 1:], rim))
    before = along(key_value, 1, evens)
    last = received[GROUP - 1 :, 1:]
    edge = along(last, 2, odds) + along(last, 1, odds)
    base = pl.pallas_call(
        hyena_kernel,
        out_shape=jax.ShapeDtypeStruct((rows, width), jnp.float32),
        in_specs=[SMEM, VMEM, VMEM, VMEM, VMEM],
        out_specs=VMEM,
        scratch_shapes=[pltpu.VMEM((rows + 16, width), jnp.float32)],
        cost_estimate=cost(2000),
        name="hyena",
    )(starts, residual, streams, rim, taps)
    key_value, base = lax.optimization_barrier((key_value, base))
    other = lax.ppermute(key_value, "core", swap)
    state = attend(long_chip, 0, starts, received, other)
    edge_other = lax.ppermute(edge, "core", swap)
    before, edge, edge_other, state = lax.optimization_barrier((before, edge, edge_other, state))
    before_other = lax.ppermute(before, "core", swap)
    state = attend(long_chip, 1, starts, received, before, edge, *state)
    out = attend(long_chip, 2, starts, received, before_other, edge_other, *state)
    out = out.astype(jnp.float16)
    heads = lax.all_to_all(out, "z", 0, 0, axis_index_groups=groups, tiled=True)
    return base, heads.astype(jnp.float32)


def on_device(
    residual,
    hyena_streams,
    hyena_filter,
    attention_streams,
    norm_gain,
    record_starts,
    record_lengths,
    segment_ids,
):
    rows, width = residual.shape
    records = record_starts.shape[0]
    seq, mp = lax.axis_size(POSITIONS), lax.axis_size("mp")
    packed, lines, chip = pack(record_starts, record_lengths, attention_streams.transpose(1, 0, 2))
    base, heads = lax.switch(
        chip[0],
        [functools.partial(mixers, here) for here in range(CHIPS - LONG // (2 * rows) + 1)],
        packed,
        residual,
        hyena_streams.transpose(1, 0, 2),
        hyena_filter,
        record_starts,
    )

    with jax.named_scope("mean_square"):
        stream, squares = pl.pallas_call(
            stream_kernel,
            out_shape=(
                jax.ShapeDtypeStruct((rows, width), jnp.float32),
                jax.ShapeDtypeStruct((mp, 1, rows), jnp.float32),
            ),
            name="stream",
        )(base, heads)
        parts = lax.all_to_all(squares, "mp", 0, 0, tiled=True)
    with jax.named_scope("record_energy"):
        mean, sums = pl.pallas_call(
            records_kernel,
            out_shape=(
                jax.ShapeDtypeStruct((rows, rows), jnp.float32),
                jax.ShapeDtypeStruct((seq, 1, 128), jnp.float32),
            ),
            name="records",
        )(lines, parts)
        sums = lax.all_to_all(sums, POSITIONS, 0, 0, tiled=True)
        record_energy = jnp.sum(sums, axis=(0, 1))[:records] / record_lengths.astype(jnp.float32)
    mixed = pl.pallas_call(
        scale_kernel,
        out_shape=jax.ShapeDtypeStruct((rows, width), jnp.float32),
        cost_estimate=cost(1000),
        name="scale",
    )(stream, mean, norm_gain[None, :])
    return (mixed, record_energy)


def solution(mesh):
    fine = Mesh(mesh.devices.reshape(CHIPS, 2, mesh.shape["mp"]), ("z", "core", "mp"))
    return jax.shard_map(
        on_device,
        mesh=fine,
        in_specs=(
            P(POSITIONS, "mp"),
            P(POSITIONS, None, "mp"),
            P(None, "mp"),
            P(POSITIONS, None, "mp"),
            P("mp"),
            P(),
            P(),
            P(POSITIONS),
        ),
        out_specs=(P(POSITIONS, "mp"), P()),
        check_vma=False,
    )
```

```python
import functools

import jax
import jax.numpy as jnp
from jax import lax
from jax.experimental import pallas as pl
from jax.experimental.pallas import tpu as pltpu
from jax.sharding import Mesh
from jax.sharding import PartitionSpec as P

D = 8192
HEAD_DIM = 128
GROUP = 4
MASKED = -1e30
SCALE = HEAD_DIM**-0.5 * 1.4426950408889634
POSITIONS = ("z", "core")
CHIPS = 16
LONG = 2048
SMEM = pl.BlockSpec(memory_space=pltpu.SMEM)
VMEM = pl.BlockSpec(memory_space=pltpu.VMEM)


def cost(nanoseconds):
    return pl.CostEstimate(flops=nanoseconds * 1_000_000, bytes_accessed=1 << 20, transcendentals=0)


def as_line(scalars):
    lane = lax.broadcasted_iota(jnp.int32, (1, HEAD_DIM), 1)
    line = jnp.zeros((1, HEAD_DIM), jnp.int32)
    for record in range(scalars.shape[0]):
        line = jnp.where(lane == record, scalars[record], line)
    return line


def pack_kernel(starts, lengths, x_ref, out_ref, lines_ref, chip_ref):
    for head in range(GROUP):
        for stream in range(3):
            out_ref[head, stream] = x_ref[stream, :, head * HEAD_DIM : (head + 1) * HEAD_DIM]
    long_start = jnp.int32(0)
    for record in range(starts.shape[0]):
        long_start = jnp.where(lengths[record] == LONG, starts[record], long_start)
    chip_ref[0] = long_start // (2 * x_ref.shape[1])
    lines_ref[0] = as_line(starts)
    lines_ref[1] = as_line(lengths)


def pack(starts, lengths, streams):
    rows = streams.shape[1]
    return pl.pallas_call(
        pack_kernel,
        out_shape=(
            jax.ShapeDtypeStruct((GROUP, 3, rows, HEAD_DIM), streams.dtype),
            jax.ShapeDtypeStruct((2, 1, HEAD_DIM), jnp.int32),
            jax.ShapeDtypeStruct((1,), jnp.int32),
        ),
        in_specs=[SMEM, SMEM, VMEM],
        out_specs=(VMEM, VMEM, SMEM),
        name="pack_heads",
    )(starts, lengths, streams)


def cut_of(long_chip):
    return (long_chip + 1) % GROUP, (long_chip + 1) // GROUP % 2


def group_of(cut):
    return lax.rem(lax.axis_index("z") + CHIPS - cut, CHIPS) // GROUP


def attend_rows(q, query_pos, row_start, sources, state, causal=True):
    rows = q.shape[0]
    scores = []
    for keys, _, first in sources:
        s = lax.dot_general(q, keys, (((1,), (1,)), ((), ())), preferred_element_type=jnp.float32)
        key_pos = jnp.concatenate(
            [here + lax.broadcasted_iota(jnp.int32, (1, rows), 1) for here in first], axis=1
        )
        allowed = key_pos >= row_start
        if causal:
            allowed = allowed & (key_pos <= query_pos)
        scores.append(jnp.where(allowed, s * SCALE, MASKED))
    top = functools.reduce(jnp.maximum, [jnp.max(s, axis=1, keepdims=True) for s in scores])
    if state is not None:
        top = jnp.maximum(top, state[0])
    total = jnp.zeros((rows, 1), jnp.float32)
    summed = jnp.zeros((rows, HEAD_DIM), jnp.float32)
    for s, (_, values, _) in zip(scores, sources):
        weights = jnp.exp2(s - top)
        total = total + jnp.sum(weights, axis=1, keepdims=True)
        summed = summed + jnp.dot(
            weights.astype(jnp.bfloat16), values, preferred_element_type=jnp.float32
        )
    if state is not None:
        factor = jnp.exp2(state[0] - top)
        total = total + state[1] * factor
        summed = summed + state[2] * factor
    return top, total, summed


def chip_position(cut, group, place, core, rows):
    chip = lax.rem(group * GROUP + place + (cut + 2 * CHIPS), CHIPS)
    return (chip * 2 + core) * rows


def blocks_of(ref, low, high, offset=0):
    rows = ref.shape[2]
    return [ref[low:high, offset + i].reshape((high - low) * rows, HEAD_DIM) for i in range(2)]


def attend_kernel(long_chip, phase, starts, q_ref, *refs):
    cut, even = cut_of(long_chip)
    group, core = group_of(cut), lax.axis_index("core")
    rows = q_ref.shape[2]
    place = lax.broadcasted_iota(jnp.int32, (rows, 1), 0)

    is_even = lax.rem(group + even, 2) == 0

    def own(ref, of_core, count, offset=0):
        blocks = blocks_of(ref, 0, count, offset)
        return *blocks, [chip_position(cut, group, i, of_core, rows) for i in range(count)]

    def before(ref, of_core):
        first = [chip_position(cut, group - 1, i, of_core, rows) for i in range(GROUP)]
        return *blocks_of(ref, 0, GROUP), [jnp.where(is_even, -2 * LONG, here) for here in first]

    def edge(ref, of_core):
        back = jnp.where(is_even, 1, 2)
        return ref[0, 0], ref[0, 1], [chip_position(cut, group - back, GROUP - 1, of_core, rows)]

    if phase == 0:
        other, edge_ref, edge_other, *outs = refs
        sources = [own(q_ref, core, GROUP, 1), own(other, 1 - core, GROUP)]
        sources += [edge(edge_ref, core), edge(edge_other, 1 - core)]
    else:
        sources = [before(refs[0], core if phase == 1 else 1 - core)]
        state, outs = refs[1:4], refs[4:]

    @pl.loop(0, GROUP)
    def _(block):
        query_first = chip_position(cut, group, block, core, rows)
        query_pos = query_first + place
        here = sources
        if phase > 0:
            ((keys, values, firsts),) = sources
            firsts = [jnp.where(first < query_first, first, -2 * LONG) for first in firsts]
            here = [(keys, values, firsts)]
        top, total, summed = attend_rows(
            q_ref[block, 0],
            query_pos,
            row_starts(starts, query_pos),
            here,
            None if phase == 0 else [ref[block] for ref in state],
            causal=phase == 0,
        )
        if phase < 2:
            outs[0][block], outs[1][block], outs[2][block] = top, total, summed
        else:
            outs[0][block] = summed / total


def attend(long_chip, phase, starts, received, *others):
    rows = received.shape[2]
    column = jax.ShapeDtypeStruct((GROUP, rows, 1), jnp.float32)
    full = jax.ShapeDtypeStruct((GROUP, rows, HEAD_DIM), jnp.float32)
    return pl.pallas_call(
        functools.partial(attend_kernel, long_chip, phase),
        out_shape=full if phase == 2 else (column, column, full),
        in_specs=[SMEM] + [VMEM] * (1 + len(others)),
        compiler_params=pltpu.CompilerParams(vmem_limit_bytes=32 * 1024 * 1024),
        cost_estimate=cost(2000 if phase else 10),
        name=f"attend{phase}",
    )(starts, received, *others)


def row_starts(starts, positions):
    found = jnp.zeros_like(positions)
    for record in range(starts.shape[0]):
        here = starts[record]
        found = jnp.where(positions >= here, here, found)
    return found


def hyena_kernel(starts, residual, streams, rim, taps_ref, out_ref, padded):
    rows = residual.shape[0]
    edge = rim.shape[1]
    taps = taps_ref.shape[0]
    positions = lax.axis_index(POSITIONS) * rows + lax.broadcasted_iota(jnp.int32, (rows, 1), 0)
    first = row_starts(starts, positions)
    padded[:edge] = rim[0].astype(jnp.float32) * rim[1].astype(jnp.float32)
    padded[edge:] = streams[1].astype(jnp.float32) * streams[2].astype(jnp.float32)
    filtered = jnp.zeros(out_ref.shape, jnp.float32)
    for tap in range(taps):
        term = taps_ref[tap : tap + 1, :] * padded[edge - tap : edge - tap + rows]
        filtered = filtered + jnp.where(positions - tap >= first, term, 0.0)
    out_ref[...] = residual[...].astype(jnp.float32) + streams[0].astype(jnp.float32) * filtered


def stream_kernel(base, heads, stream_ref, squares_ref):
    rows = base.shape[0]
    squares = jnp.zeros((rows, HEAD_DIM), jnp.float32)
    for head in range(GROUP):
        columns = slice(head * HEAD_DIM, (head + 1) * HEAD_DIM)
        value = base[:, columns] + heads[head]
        stream_ref[:, columns] = value
        squares = squares + value * value
    line = jnp.sum(squares.T, axis=0, keepdims=True)
    for device in range(squares_ref.shape[0]):
        squares_ref[device] = line


def records_kernel(lines, parts, mean_ref, sums_ref):
    rows = parts.shape[2]
    line = jnp.sum(parts[:, 0, :], axis=0, keepdims=True) / D
    mean = jnp.broadcast_to(line, (rows, rows)).T
    mean_ref[...] = mean
    position = lax.axis_index(POSITIONS) * rows + lax.broadcasted_iota(jnp.int32, (rows, rows), 0)
    first = lines[0]
    inside = (position >= first) & (position < first + lines[1])
    sums = jnp.sum(jnp.where(inside, mean, 0.0), axis=0, keepdims=True)
    for device in range(sums_ref.shape[0]):
        sums_ref[device] = sums


def scale_kernel(stream, mean, gain, out_ref):
    factor = lax.rsqrt(mean[...] + 1e-05)
    for head in range(GROUP):
        columns = slice(head * HEAD_DIM, (head + 1) * HEAD_DIM)
        out_ref[:, columns] = stream[:, columns] * factor * gain[:, columns]


def mixers(long_chip, packed, residual, streams, taps, starts):
    rows, width = residual.shape
    cut, even = cut_of(long_chip)
    seq = lax.axis_size(POSITIONS)
    groups = [
        [(cut + GROUP * k + i) % CHIPS for i in range(GROUP)] for k in range(CHIPS // GROUP)
    ]
    swap = [(0, 1), (1, 0)]

    def along(value, count, of_groups):
        pairs = [(i, (i + count * GROUP) % CHIPS) for k in of_groups for i in groups[k]]
        return lax.ppermute(value, "z", pairs)

    evens, odds = [even, even + 2], [1 - even, 3 - even]
    rim = lax.ppermute(streams[1:, rows - 16 :], POSITIONS, [(i, i + 1) for i in range(seq - 1)])
    received = lax.all_to_all(packed, "z", 0, 0, axis_index_groups=groups, tiled=True)
    key_value, rim = lax.optimization_barrier((received[:, 1:], rim))
    before = along(key_value, 1, evens)
    last = received[GROUP - 1 :, 1:]
    other = lax.ppermute(key_value, "core", swap)
    last, streams, other = lax.optimization_barrier((last, streams, other))
    edge = along(last, 2, odds) + along(last, 1, odds)
    base = pl.pallas_call(
        hyena_kernel,
        out_shape=jax.ShapeDtypeStruct((rows, width), jnp.float32),
        in_specs=[SMEM, VMEM, VMEM, VMEM, VMEM],
        out_specs=VMEM,
        scratch_shapes=[pltpu.VMEM((rows + 16, width), jnp.float32)],
        cost_estimate=cost(10),
        name="hyena",
    )(starts, residual, streams, rim, taps)
    edge_other = lax.ppermute(edge, "core", swap)
    state = attend(long_chip, 0, starts, received, other, edge, edge_other)
    before, state, base = lax.optimization_barrier((before, state, base))
    before_other = lax.ppermute(before, "core", swap)
    state = attend(long_chip, 1, starts, received, before, *state)
    out = attend(long_chip, 2, starts, received, before_other, *state)
    out = out.astype(jnp.float16)
    heads = lax.all_to_all(out, "z", 0, 0, axis_index_groups=groups, tiled=True)
    return base, heads.astype(jnp.float32)


def on_device(
    residual,
    hyena_streams,
    hyena_filter,
    attention_streams,
    norm_gain,
    record_starts,
    record_lengths,
    segment_ids,
):
    rows, width = residual.shape
    records = record_starts.shape[0]
    seq, mp = lax.axis_size(POSITIONS), lax.axis_size("mp")
    packed, lines, chip = pack(record_starts, record_lengths, attention_streams.transpose(1, 0, 2))
    base, heads = lax.switch(
        chip[0],
        [functools.partial(mixers, here) for here in range(CHIPS - LONG // (2 * rows) + 1)],
        packed,
        residual,
        hyena_streams.transpose(1, 0, 2),
        hyena_filter,
        record_starts,
    )

    with jax.named_scope("mean_square"):
        stream, squares = pl.pallas_call(
            stream_kernel,
            out_shape=(
                jax.ShapeDtypeStruct((rows, width), jnp.float32),
                jax.ShapeDtypeStruct((mp, 1, rows), jnp.float32),
            ),
            name="stream",
        )(base, heads)
        parts = lax.all_to_all(squares, "mp", 0, 0, tiled=True)
    with jax.named_scope("record_energy"):
        mean, sums = pl.pallas_call(
            records_kernel,
            out_shape=(
                jax.ShapeDtypeStruct((rows, rows), jnp.float32),
                jax.ShapeDtypeStruct((seq, 1, 128), jnp.float32),
            ),
            name="records",
        )(lines, parts)
        sums = lax.all_to_all(sums, POSITIONS, 0, 0, tiled=True)
        record_energy = jnp.sum(sums, axis=(0, 1))[:records] / record_lengths.astype(jnp.float32)
    mixed = pl.pallas_call(
        scale_kernel,
        out_shape=jax.ShapeDtypeStruct((rows, width), jnp.float32),
        cost_estimate=cost(1000),
        name="scale",
    )(stream, mean, norm_gain[None, :])
    return (mixed, record_energy)


def solution(mesh):
    fine = Mesh(mesh.devices.reshape(CHIPS, 2, mesh.shape["mp"]), ("z", "core", "mp"))
    return jax.shard_map(
        on_device,
        mesh=fine,
        in_specs=(
            P(POSITIONS, "mp"),
            P(POSITIONS, None, "mp"),
            P(None, "mp"),
            P(POSITIONS, None, "mp"),
            P("mp"),
            P(),
            P(),
            P(POSITIONS),
        ),
        out_specs=(P(POSITIONS, "mp"), P()),
        check_vma=False,
    )
```

```python
import functools

import jax
import jax.numpy as jnp
from jax import lax
from jax.experimental import pallas as pl
from jax.experimental.pallas import tpu as pltpu
from jax.sharding import Mesh
from jax.sharding import PartitionSpec as P

D = 8192
HEAD_DIM = 128
GROUP = 4
MASKED = -1e30
SCALE = HEAD_DIM**-0.5 * 1.4426950408889634
POSITIONS = ("z", "core")
CHIPS = 16
LONG = 2048
SMEM = pl.BlockSpec(memory_space=pltpu.SMEM)
VMEM = pl.BlockSpec(memory_space=pltpu.VMEM)


def cost(nanoseconds):
    return pl.CostEstimate(flops=nanoseconds * 1_000_000, bytes_accessed=1 << 20, transcendentals=0)


def as_line(scalars):
    lane = lax.broadcasted_iota(jnp.int32, (1, HEAD_DIM), 1)
    line = jnp.zeros((1, HEAD_DIM), jnp.int32)
    for record in range(scalars.shape[0]):
        line = jnp.where(lane == record, scalars[record], line)
    return line


def pack_kernel(starts, lengths, x_ref, out_ref, lines_ref, chip_ref):
    for head in range(GROUP):
        for stream in range(3):
            out_ref[head, stream] = x_ref[stream, :, head * HEAD_DIM : (head + 1) * HEAD_DIM]
    long_start = jnp.int32(0)
    for record in range(starts.shape[0]):
        long_start = jnp.where(lengths[record] == LONG, starts[record], long_start)
    chip_ref[0] = long_start // (2 * x_ref.shape[1])
    lines_ref[0] = as_line(starts)
    lines_ref[1] = as_line(lengths)


def pack(starts, lengths, streams):
    rows = streams.shape[1]
    return pl.pallas_call(
        pack_kernel,
        out_shape=(
            jax.ShapeDtypeStruct((GROUP, 3, rows, HEAD_DIM), streams.dtype),
            jax.ShapeDtypeStruct((2, 1, HEAD_DIM), jnp.int32),
            jax.ShapeDtypeStruct((1,), jnp.int32),
        ),
        in_specs=[SMEM, SMEM, VMEM],
        out_specs=(VMEM, VMEM, SMEM),
        name="pack_heads",
    )(starts, lengths, streams)


def cut_of(long_chip):
    return (long_chip + 1) % GROUP, (long_chip + 1) // GROUP % 2


def group_of(cut):
    return lax.rem(lax.axis_index("z") + CHIPS - cut, CHIPS) // GROUP


def attend_rows(q, query_pos, row_start, sources, state, causal=True):
    rows = q.shape[0]
    scores = []
    for keys, _, first in sources:
        s = lax.dot_general(q, keys, (((1,), (1,)), ((), ())), preferred_element_type=jnp.float32)
        key_pos = jnp.concatenate(
            [here + lax.broadcasted_iota(jnp.int32, (1, rows), 1) for here in first], axis=1
        )
        allowed = key_pos >= row_start
        if causal:
            allowed = allowed & (key_pos <= query_pos)
        scores.append(jnp.where(allowed, s * SCALE, MASKED))
    top = functools.reduce(jnp.maximum, [jnp.max(s, axis=1, keepdims=True) for s in scores])
    if state is not None:
        top = jnp.maximum(top, state[0])
    total = jnp.zeros((rows, 1), jnp.float32)
    summed = jnp.zeros((rows, HEAD_DIM), jnp.float32)
    for s, (_, values, _) in zip(scores, sources):
        weights = jnp.exp2(s - top)
        total = total + jnp.sum(weights, axis=1, keepdims=True)
        summed = summed + jnp.dot(
            weights.astype(jnp.bfloat16), values, preferred_element_type=jnp.float32
        )
    if state is not None:
        factor = jnp.exp2(state[0] - top)
        total = total + state[1] * factor
        summed = summed + state[2] * factor
    return top, total, summed


def chip_position(cut, group, place, core, rows):
    chip = lax.rem(group * GROUP + place + (cut + 2 * CHIPS), CHIPS)
    return (chip * 2 + core) * rows


def blocks_of(ref, low, high, offset=0):
    rows = ref.shape[2]
    return [ref[low:high, offset + i].reshape((high - low) * rows, HEAD_DIM) for i in range(2)]


def attend_kernel(long_chip, phase, starts, q_ref, *refs):
    cut, even = cut_of(long_chip)
    group, core = group_of(cut), lax.axis_index("core")
    rows = q_ref.shape[2]
    place = lax.broadcasted_iota(jnp.int32, (rows, 1), 0)

    is_even = lax.rem(group + even, 2) == 0

    def own(ref, of_core, count, offset=0):
        blocks = blocks_of(ref, 0, count, offset)
        return *blocks, [chip_position(cut, group, i, of_core, rows) for i in range(count)]

    def before(ref, of_core):
        first = [chip_position(cut, group - 1, i, of_core, rows) for i in range(GROUP)]
        return *blocks_of(ref, 0, GROUP), [jnp.where(is_even, -2 * LONG, here) for here in first]

    def edge(ref, of_core):
        back = jnp.where(is_even, 1, 2)
        return ref[0, 0], ref[0, 1], [chip_position(cut, group - back, GROUP - 1, of_core, rows)]

    if phase == 0:
        other, edge_ref, edge_other, *outs = refs
        sources = [own(q_ref, core, GROUP, 1), own(other, 1 - core, GROUP)]
        sources += [edge(edge_ref, core), edge(edge_other, 1 - core)]
    else:
        sources = [before(refs[0], core if phase == 1 else 1 - core)]
        state, outs = refs[1:4], refs[4:]

    @pl.loop(0, GROUP, unroll=2 if phase else 1)
    def _(block):
        query_first = chip_position(cut, group, block, core, rows)
        query_pos = query_first + place
        here = sources
        if phase > 0:
            ((keys, values, firsts),) = sources
            firsts = [jnp.where(first < query_first, first, -2 * LONG) for first in firsts]
            here = [(keys, values, firsts)]
        top, total, summed = attend_rows(
            q_ref[block, 0],
            query_pos,
            row_starts(starts, query_pos),
            here,
            None if phase == 0 else [ref[block] for ref in state],
            causal=phase == 0,
        )
        if phase < 2:
            outs[0][block], outs[1][block], outs[2][block] = top, total, summed
        else:
            outs[0][block] = summed / total


def attend(long_chip, phase, starts, received, *others):
    rows = received.shape[2]
    column = jax.ShapeDtypeStruct((GROUP, rows, 1), jnp.float32)
    full = jax.ShapeDtypeStruct((GROUP, rows, HEAD_DIM), jnp.float32)
    return pl.pallas_call(
        functools.partial(attend_kernel, long_chip, phase),
        out_shape=full if phase == 2 else (column, column, full),
        in_specs=[SMEM] + [VMEM] * (1 + len(others)),
        compiler_params=pltpu.CompilerParams(vmem_limit_bytes=32 * 1024 * 1024),
        cost_estimate=cost(2000 if phase else 10),
        name=f"attend{phase}",
    )(starts, received, *others)


def row_starts(starts, positions):
    found = jnp.zeros_like(positions)
    for record in range(starts.shape[0]):
        here = starts[record]
        found = jnp.where(positions >= here, here, found)
    return found


def hyena_kernel(starts, residual, streams, rim, taps_ref, out_ref, padded):
    rows = residual.shape[0]
    edge = rim.shape[1]
    taps = taps_ref.shape[0]
    positions = lax.axis_index(POSITIONS) * rows + lax.broadcasted_iota(jnp.int32, (rows, 1), 0)
    first = row_starts(starts, positions)
    padded[:edge] = rim[0].astype(jnp.float32) * rim[1].astype(jnp.float32)
    padded[edge:] = streams[1].astype(jnp.float32) * streams[2].astype(jnp.float32)
    filtered = jnp.zeros(out_ref.shape, jnp.float32)
    for tap in range(taps):
        term = taps_ref[tap : tap + 1, :] * padded[edge - tap : edge - tap + rows]
        filtered = filtered + jnp.where(positions - tap >= first, term, 0.0)
    out_ref[...] = residual[...].astype(jnp.float32) + streams[0].astype(jnp.float32) * filtered


def stream_kernel(base, heads, stream_ref, squares_ref):
    rows = base.shape[0]
    squares = jnp.zeros((rows, HEAD_DIM), jnp.float32)
    for head in range(GROUP):
        columns = slice(head * HEAD_DIM, (head + 1) * HEAD_DIM)
        value = base[:, columns] + heads[head]
        stream_ref[:, columns] = value
        squares = squares + value * value
    line = jnp.sum(squares.T, axis=0, keepdims=True)
    for device in range(squares_ref.shape[0]):
        squares_ref[device] = line


def records_kernel(lines, parts, mean_ref, sums_ref):
    rows = parts.shape[2]
    line = jnp.sum(parts[:, 0, :], axis=0, keepdims=True) / D
    mean = jnp.broadcast_to(line, (rows, rows)).T
    mean_ref[...] = mean
    position = lax.axis_index(POSITIONS) * rows + lax.broadcasted_iota(jnp.int32, (rows, rows), 0)
    first = lines[0]
    inside = (position >= first) & (position < first + lines[1])
    sums = jnp.sum(jnp.where(inside, mean, 0.0), axis=0, keepdims=True)
    for device in range(sums_ref.shape[0]):
        sums_ref[device] = sums


def scale_kernel(stream, mean, gain, out_ref):
    factor = lax.rsqrt(mean[...] + 1e-05)
    for head in range(GROUP):
        columns = slice(head * HEAD_DIM, (head + 1) * HEAD_DIM)
        out_ref[:, columns] = stream[:, columns] * factor * gain[:, columns]


def mixers(long_chip, packed, residual, streams, taps, starts):
    rows, width = residual.shape
    cut, even = cut_of(long_chip)
    seq = lax.axis_size(POSITIONS)
    groups = [
        [(cut + GROUP * k + i) % CHIPS for i in range(GROUP)] for k in range(CHIPS // GROUP)
    ]
    swap = [(0, 1), (1, 0)]

    def along(value, count, of_groups):
        pairs = [(i, (i + count * GROUP) % CHIPS) for k in of_groups for i in groups[k]]
        return lax.ppermute(value, "z", pairs)

    evens, odds = [even, even + 2], [1 - even, 3 - even]
    rim = lax.ppermute(streams[1:, rows - 16 :], POSITIONS, [(i, i + 1) for i in range(seq - 1)])
    received = lax.all_to_all(packed, "z", 0, 0, axis_index_groups=groups, tiled=True)
    key_value, rim = lax.optimization_barrier((received[:, 1:], rim))
    before = along(key_value, 1, evens)
    last = received[GROUP - 1 :, 1:]
    other = lax.ppermute(key_value, "core", swap)
    edge = along(last, 2, odds) + along(last, 1, odds)
    base = pl.pallas_call(
        hyena_kernel,
        out_shape=jax.ShapeDtypeStruct((rows, width), jnp.float32),
        in_specs=[SMEM, VMEM, VMEM, VMEM, VMEM],
        out_specs=VMEM,
        scratch_shapes=[pltpu.VMEM((rows + 16, width), jnp.float32)],
        cost_estimate=cost(10),
        name="hyena",
    )(starts, residual, streams, rim, taps)
    edge_other = lax.ppermute(edge, "core", swap)
    state = attend(long_chip, 0, starts, received, other, edge, edge_other)
    before, state, base = lax.optimization_barrier((before, state, base))
    before_other = lax.ppermute(before, "core", swap)
    state = attend(long_chip, 1, starts, received, before, *state)
    out = attend(long_chip, 2, starts, received, before_other, *state)
    out = out.astype(jnp.float16)
    heads = lax.all_to_all(out, "z", 0, 0, axis_index_groups=groups, tiled=True)
    return base, heads.astype(jnp.float32)


def on_device(
    residual,
    hyena_streams,
    hyena_filter,
    attention_streams,
    norm_gain,
    record_starts,
    record_lengths,
    segment_ids,
):
    rows, width = residual.shape
    records = record_starts.shape[0]
    seq, mp = lax.axis_size(POSITIONS), lax.axis_size("mp")
    packed, lines, chip = pack(record_starts, record_lengths, attention_streams.transpose(1, 0, 2))
    base, heads = lax.switch(
        chip[0],
        [functools.partial(mixers, here) for here in range(CHIPS - LONG // (2 * rows) + 1)],
        packed,
        residual,
        hyena_streams.transpose(1, 0, 2),
        hyena_filter,
        record_starts,
    )

    with jax.named_scope("mean_square"):
        stream, squares = pl.pallas_call(
            stream_kernel,
            out_shape=(
                jax.ShapeDtypeStruct((rows, width), jnp.float32),
                jax.ShapeDtypeStruct((mp, 1, rows), jnp.float32),
            ),
            name="stream",
        )(base, heads)
        parts = lax.all_to_all(squares, "mp", 0, 0, tiled=True)
    with jax.named_scope("record_energy"):
        mean, sums = pl.pallas_call(
            records_kernel,
            out_shape=(
                jax.ShapeDtypeStruct((rows, rows), jnp.float32),
                jax.ShapeDtypeStruct((seq, 1, 128), jnp.float32),
            ),
            name="records",
        )(lines, parts)
        sums = lax.all_to_all(sums, POSITIONS, 0, 0, tiled=True)
        record_energy = jnp.sum(sums, axis=(0, 1))[:records] / record_lengths.astype(jnp.float32)
    mixed = pl.pallas_call(
        scale_kernel,
        out_shape=jax.ShapeDtypeStruct((rows, width), jnp.float32),
        cost_estimate=cost(1000),
        name="scale",
    )(stream, mean, norm_gain[None, :])
    return (mixed, record_energy)


def solution(mesh):
    fine = Mesh(mesh.devices.reshape(CHIPS, 2, mesh.shape["mp"]), ("z", "core", "mp"))
    return jax.shard_map(
        on_device,
        mesh=fine,
        in_specs=(
            P(POSITIONS, "mp"),
            P(POSITIONS, None, "mp"),
            P(None, "mp"),
            P(POSITIONS, None, "mp"),
            P("mp"),
            P(),
            P(),
            P(POSITIONS),
        ),
        out_specs=(P(POSITIONS, "mp"), P()),
        check_vma=False,
    )
```

```python
import functools

import jax
import jax.numpy as jnp
from jax import lax
from jax.experimental import pallas as pl
from jax.experimental.pallas import tpu as pltpu
from jax.sharding import Mesh
from jax.sharding import PartitionSpec as P

D = 8192
HEAD_DIM = 128
GROUP = 4
MASKED = -1e30
SCALE = HEAD_DIM**-0.5 * 1.4426950408889634
POSITIONS = ("z", "core")
CHIPS = 16
LONG = 2048
SMEM = pl.BlockSpec(memory_space=pltpu.SMEM)
VMEM = pl.BlockSpec(memory_space=pltpu.VMEM)


def cost(nanoseconds):
    return pl.CostEstimate(flops=nanoseconds * 1_000_000, bytes_accessed=1 << 20, transcendentals=0)


def as_line(scalars):
    lane = lax.broadcasted_iota(jnp.int32, (1, HEAD_DIM), 1)
    line = jnp.zeros((1, HEAD_DIM), jnp.int32)
    for record in range(scalars.shape[0]):
        line = jnp.where(lane == record, scalars[record], line)
    return line


def pack_kernel(starts, lengths, x_ref, out_ref, lines_ref, chip_ref):
    for head in range(GROUP):
        for stream in range(3):
            out_ref[head, stream] = x_ref[stream, :, head * HEAD_DIM : (head + 1) * HEAD_DIM]
    long_start = jnp.int32(0)
    for record in range(starts.shape[0]):
        long_start = jnp.where(lengths[record] == LONG, starts[record], long_start)
    chip_ref[0] = long_start // (2 * x_ref.shape[1])
    lines_ref[0] = as_line(starts)
    lines_ref[1] = as_line(lengths)


def pack(starts, lengths, streams):
    rows = streams.shape[1]
    return pl.pallas_call(
        pack_kernel,
        out_shape=(
            jax.ShapeDtypeStruct((GROUP, 3, rows, HEAD_DIM), streams.dtype),
            jax.ShapeDtypeStruct((2, 1, HEAD_DIM), jnp.int32),
            jax.ShapeDtypeStruct((1,), jnp.int32),
        ),
        in_specs=[SMEM, SMEM, VMEM],
        out_specs=(VMEM, VMEM, SMEM),
        name="pack_heads",
    )(starts, lengths, streams)


def cut_of(long_chip):
    return (long_chip + 1) % GROUP, (long_chip + 1) // GROUP % 2


def group_of(cut):
    return lax.rem(lax.axis_index("z") + CHIPS - cut, CHIPS) // GROUP


def attend_rows(q, query_pos, row_start, sources, state, causal=True):
    rows = q.shape[0]
    scores = []
    for keys, _, first in sources:
        s = lax.dot_general(q, keys, (((1,), (1,)), ((), ())), preferred_element_type=jnp.float32)
        key_pos = jnp.concatenate(
            [here + lax.broadcasted_iota(jnp.int32, (1, rows), 1) for here in first], axis=1
        )
        allowed = key_pos >= row_start
        if causal:
            allowed = allowed & (key_pos <= query_pos)
        scores.append(jnp.where(allowed, s * SCALE, MASKED))
    top = functools.reduce(jnp.maximum, [jnp.max(s, axis=1, keepdims=True) for s in scores])
    if state is not None:
        top = jnp.maximum(top, state[0])
    total = jnp.zeros((rows, 1), jnp.float32)
    summed = jnp.zeros((rows, HEAD_DIM), jnp.float32)
    for s, (_, values, _) in zip(scores, sources):
        weights = jnp.exp2(s - top)
        total = total + jnp.sum(weights, axis=1, keepdims=True)
        summed = summed + jnp.dot(
            weights.astype(jnp.bfloat16), values, preferred_element_type=jnp.float32
        )
    if state is not None:
        factor = jnp.exp2(state[0] - top)
        total = total + state[1] * factor
        summed = summed + state[2] * factor
    return top, total, summed


def chip_position(cut, group, place, core, rows):
    chip = lax.rem(group * GROUP + place + (cut + 2 * CHIPS), CHIPS)
    return (chip * 2 + core) * rows


def blocks_of(ref, low, high, offset=0):
    rows = ref.shape[2]
    return [ref[low:high, offset + i].reshape((high - low) * rows, HEAD_DIM) for i in range(2)]


def attend_kernel(long_chip, phase, starts, q_ref, *refs):
    cut, even = cut_of(long_chip)
    group, core = group_of(cut), lax.axis_index("core")
    rows = q_ref.shape[2]
    place = lax.broadcasted_iota(jnp.int32, (rows, 1), 0)

    is_even = lax.rem(group + even, 2) == 0

    def own(ref, of_core, count, offset=0):
        blocks = blocks_of(ref, 0, count, offset)
        return *blocks, [chip_position(cut, group, i, of_core, rows) for i in range(count)]

    def before(ref, of_core):
        first = [chip_position(cut, group - 1, i, of_core, rows) for i in range(GROUP)]
        return *blocks_of(ref, 0, GROUP), [jnp.where(is_even, -2 * LONG, here) for here in first]

    def edge(ref, of_core):
        back = jnp.where(is_even, 1, 2)
        return ref[0, 0], ref[0, 1], [chip_position(cut, group - back, GROUP - 1, of_core, rows)]

    if phase == 0:
        other, edge_ref, edge_other, *outs = refs
        sources = [own(q_ref, core, GROUP, 1), own(other, 1 - core, GROUP)]
        sources += [edge(edge_ref, core), edge(edge_other, 1 - core)]
    else:
        sources = [before(refs[0], core if phase == 1 else 1 - core)]
        state, outs = refs[1:4], refs[4:]

    @pl.loop(0, GROUP)
    def _(block):
        query_first = chip_position(cut, group, block, core, rows)
        query_pos = query_first + place
        here = sources
        if phase > 0:
            ((keys, values, firsts),) = sources
            firsts = [jnp.where(first < query_first, first, -2 * LONG) for first in firsts]
            here = [(keys, values, firsts)]
        top, total, summed = attend_rows(
            q_ref[block, 0],
            query_pos,
            row_starts(starts, query_pos),
            here,
            None if phase == 0 else [ref[block] for ref in state],
            causal=phase == 0,
        )
        if phase < 2:
            outs[0][block], outs[1][block], outs[2][block] = top, total, summed
        else:
            outs[0][block] = summed / total


def attend(long_chip, phase, starts, received, *others):
    rows = received.shape[2]
    column = jax.ShapeDtypeStruct((GROUP, rows, 1), jnp.float32)
    full = jax.ShapeDtypeStruct((GROUP, rows, HEAD_DIM), jnp.float32)
    return pl.pallas_call(
        functools.partial(attend_kernel, long_chip, phase),
        out_shape=full if phase == 2 else (column, column, full),
        in_specs=[SMEM] + [VMEM] * (1 + len(others)),
        compiler_params=pltpu.CompilerParams(vmem_limit_bytes=32 * 1024 * 1024),
        cost_estimate=cost(2000 if phase else 10),
        name=f"attend{phase}",
    )(starts, received, *others)


def row_starts(starts, positions):
    found = jnp.zeros_like(positions)
    for record in range(starts.shape[0]):
        here = starts[record]
        found = jnp.where(positions >= here, here, found)
    return found


def hyena_kernel(starts, residual, streams, rim, taps_ref, out_ref, padded):
    rows = residual.shape[0]
    edge = rim.shape[1]
    taps = taps_ref.shape[0]
    positions = lax.axis_index(POSITIONS) * rows + lax.broadcasted_iota(jnp.int32, (rows, 1), 0)
    first = row_starts(starts, positions)
    padded[:edge] = rim[0].astype(jnp.float32) * rim[1].astype(jnp.float32)
    padded[edge:] = streams[1].astype(jnp.float32) * streams[2].astype(jnp.float32)
    filtered = jnp.zeros(out_ref.shape, jnp.float32)
    for tap in range(taps):
        term = taps_ref[tap : tap + 1, :] * padded[edge - tap : edge - tap + rows]
        filtered = filtered + jnp.where(positions - tap >= first, term, 0.0)
    out_ref[...] = residual[...].astype(jnp.float32) + streams[0].astype(jnp.float32) * filtered


def stream_kernel(base, heads, stream_ref, squares_ref):
    rows = base.shape[0]
    squares = jnp.zeros((rows, HEAD_DIM), jnp.float32)
    for head in range(GROUP):
        columns = slice(head * HEAD_DIM, (head + 1) * HEAD_DIM)
        value = base[:, columns] + heads[head]
        stream_ref[:, columns] = value
        squares = squares + value * value
    line = jnp.sum(squares.T, axis=0, keepdims=True)
    for device in range(squares_ref.shape[0]):
        squares_ref[device] = line


def records_kernel(lines, parts, mean_ref, sums_ref):
    rows = parts.shape[2]
    line = jnp.sum(parts[:, 0, :], axis=0, keepdims=True) / D
    mean = jnp.broadcast_to(line, (rows, rows)).T
    mean_ref[...] = mean
    position = lax.axis_index(POSITIONS) * rows + lax.broadcasted_iota(jnp.int32, (rows, rows), 0)
    first = lines[0]
    inside = (position >= first) & (position < first + lines[1])
    sums = jnp.sum(jnp.where(inside, mean, 0.0), axis=0, keepdims=True)
    for device in range(sums_ref.shape[0]):
        sums_ref[device] = sums


def scale_kernel(stream, mean, gain, out_ref):
    factor = lax.rsqrt(mean[...] + 1e-05)
    for head in range(GROUP):
        columns = slice(head * HEAD_DIM, (head + 1) * HEAD_DIM)
        out_ref[:, columns] = stream[:, columns] * factor * gain[:, columns]


def mixers(long_chip, packed, residual, streams, taps, starts):
    rows, width = residual.shape
    cut, even = cut_of(long_chip)
    seq = lax.axis_size(POSITIONS)
    groups = [
        [(cut + GROUP * k + i) % CHIPS for i in range(GROUP)] for k in range(CHIPS // GROUP)
    ]
    swap = [(0, 1), (1, 0)]

    def along(value, count, of_groups):
        pairs = [(i, (i + count * GROUP) % CHIPS) for k in of_groups for i in groups[k]]
        return lax.ppermute(value, "z", pairs)

    evens, odds = [even, even + 2], [1 - even, 3 - even]
    rim = lax.ppermute(streams[1:, rows - 16 :], POSITIONS, [(i, i + 1) for i in range(seq - 1)])
    received = lax.all_to_all(packed, "z", 0, 0, axis_index_groups=groups, tiled=True)
    key_value, rim = lax.optimization_barrier((received[:, 1:], rim))
    before = along(key_value, 1, evens)
    last = received[GROUP - 1 :, 1:]
    other = lax.ppermute(key_value, "core", swap)
    last, streams, other = lax.optimization_barrier((last, streams, other))
    edge = along(last, 2, odds) + along(last, 1, odds)
    base = pl.pallas_call(
        hyena_kernel,
        out_shape=jax.ShapeDtypeStruct((rows, width), jnp.float32),
        in_specs=[SMEM, VMEM, VMEM, VMEM, VMEM],
        out_specs=VMEM,
        scratch_shapes=[pltpu.VMEM((rows + 16, width), jnp.float32)],
        cost_estimate=cost(10),
        name="hyena",
    )(starts, residual, streams, rim, taps)
    edge_other = lax.ppermute(edge, "core", swap)
    state = attend(long_chip, 0, starts, received, other, edge, edge_other)
    before, state, base = lax.optimization_barrier((before, state, base))
    before_other = lax.ppermute(before, "core", swap)
    state = attend(long_chip, 1, starts, received, before, *state)
    out = attend(long_chip, 2, starts, received, before_other, *state)
    out = out.astype(jnp.float16)
    heads = lax.all_to_all(out, "z", 0, 0, axis_index_groups=groups, tiled=True)
    return base, heads.astype(jnp.float32)


def on_device(
    residual,
    hyena_streams,
    hyena_filter,
    attention_streams,
    norm_gain,
    record_starts,
    record_lengths,
    segment_ids,
):
    rows, width = residual.shape
    records = record_starts.shape[0]
    seq, mp = lax.axis_size(POSITIONS), lax.axis_size("mp")
    packed, lines, chip = pack(record_starts, record_lengths, attention_streams.transpose(1, 0, 2))
    base, heads = lax.switch(
        chip[0],
        [functools.partial(mixers, here) for here in range(CHIPS - LONG // (2 * rows) + 1)],
        packed,
        residual,
        hyena_streams.transpose(1, 0, 2),
        hyena_filter,
        record_starts,
    )

    with jax.named_scope("mean_square"):
        stream, squares = pl.pallas_call(
            stream_kernel,
            out_shape=(
                jax.ShapeDtypeStruct((rows, width), jnp.float32),
                jax.ShapeDtypeStruct((mp, 1, rows), jnp.float32),
            ),
            name="stream",
        )(base, heads)
        parts = lax.all_to_all(squares, "mp", 0, 0, tiled=True)
    with jax.named_scope("record_energy"):
        mean, sums = pl.pallas_call(
            records_kernel,
            out_shape=(
                jax.ShapeDtypeStruct((rows, rows), jnp.float32),
                jax.ShapeDtypeStruct((seq, 1, 128), jnp.float32),
            ),
            name="records",
        )(lines, parts)
        sums = lax.all_to_all(sums, ("core", "z"), 0, 0, tiled=True)
        record_energy = jnp.sum(sums, axis=(0, 1))[:records] / record_lengths.astype(jnp.float32)
    mixed = pl.pallas_call(
        scale_kernel,
        out_shape=jax.ShapeDtypeStruct((rows, width), jnp.float32),
        cost_estimate=cost(1000),
        name="scale",
    )(stream, mean, norm_gain[None, :])
    return (mixed, record_energy)


def solution(mesh):
    fine = Mesh(mesh.devices.reshape(CHIPS, 2, mesh.shape["mp"]), ("z", "core", "mp"))
    return jax.shard_map(
        on_device,
        mesh=fine,
        in_specs=(
            P(POSITIONS, "mp"),
            P(POSITIONS, None, "mp"),
            P(None, "mp"),
            P(POSITIONS, None, "mp"),
            P("mp"),
            P(),
            P(),
            P(POSITIONS),
        ),
        out_specs=(P(POSITIONS, "mp"), P()),
        check_vma=False,
    )
```

```python
import functools

import jax
import jax.numpy as jnp
from jax import lax
from jax.experimental import pallas as pl
from jax.experimental.pallas import tpu as pltpu
from jax.sharding import Mesh
from jax.sharding import PartitionSpec as P

D = 8192
HEAD_DIM = 128
GROUP = 4
MASKED = -1e30
SCALE = HEAD_DIM**-0.5 * 1.4426950408889634
POSITIONS = ("z", "core")
CHIPS = 16
LONG = 2048
SMEM = pl.BlockSpec(memory_space=pltpu.SMEM)
VMEM = pl.BlockSpec(memory_space=pltpu.VMEM)


def cost(nanoseconds):
    return pl.CostEstimate(flops=nanoseconds * 1_000_000, bytes_accessed=1 << 20, transcendentals=0)


def as_line(scalars):
    lane = lax.broadcasted_iota(jnp.int32, (1, HEAD_DIM), 1)
    line = jnp.zeros((1, HEAD_DIM), jnp.int32)
    for record in range(scalars.shape[0]):
        line = jnp.where(lane == record, scalars[record], line)
    return line


def pack_kernel(starts, lengths, x_ref, out_ref, lines_ref, chip_ref):
    for head in range(GROUP):
        for stream in range(3):
            out_ref[head, stream] = x_ref[stream, :, head * HEAD_DIM : (head + 1) * HEAD_DIM]
    long_start = jnp.int32(0)
    for record in range(starts.shape[0]):
        long_start = jnp.where(lengths[record] == LONG, starts[record], long_start)
    chip_ref[0] = long_start // (2 * x_ref.shape[1])
    lines_ref[0] = as_line(starts)
    lines_ref[1] = as_line(lengths)


def pack(starts, lengths, streams):
    rows = streams.shape[1]
    return pl.pallas_call(
        pack_kernel,
        out_shape=(
            jax.ShapeDtypeStruct((GROUP, 3, rows, HEAD_DIM), streams.dtype),
            jax.ShapeDtypeStruct((2, 1, HEAD_DIM), jnp.int32),
            jax.ShapeDtypeStruct((1,), jnp.int32),
        ),
        in_specs=[SMEM, SMEM, VMEM],
        out_specs=(VMEM, VMEM, SMEM),
        name="pack_heads",
    )(starts, lengths, streams)


def cut_of(long_chip):
    return (long_chip + 1) % GROUP, (long_chip + 1) // GROUP % 2


def group_of(cut):
    return lax.rem(lax.axis_index("z") + CHIPS - cut, CHIPS) // GROUP


def attend_rows(q, query_pos, row_start, sources, state, causal=True):
    rows = q.shape[0]
    scores = []
    for keys, _, first in sources:
        s = lax.dot_general(q, keys, (((1,), (1,)), ((), ())), preferred_element_type=jnp.float32)
        key_pos = jnp.concatenate(
            [here + lax.broadcasted_iota(jnp.int32, (1, rows), 1) for here in first], axis=1
        )
        allowed = key_pos >= row_start
        if causal:
            allowed = allowed & (key_pos <= query_pos)
        scores.append(jnp.where(allowed, s * SCALE, MASKED))
    top = functools.reduce(jnp.maximum, [jnp.max(s, axis=1, keepdims=True) for s in scores])
    if state is not None:
        top = jnp.maximum(top, state[0])
    total = jnp.zeros((rows, 1), jnp.float32)
    summed = jnp.zeros((rows, HEAD_DIM), jnp.float32)
    for s, (_, values, _) in zip(scores, sources):
        weights = jnp.exp2(s - top)
        total = total + jnp.sum(weights, axis=1, keepdims=True)
        summed = summed + jnp.dot(
            weights.astype(jnp.bfloat16), values, preferred_element_type=jnp.float32
        )
    if state is not None:
        factor = jnp.exp2(state[0] - top)
        total = total + state[1] * factor
        summed = summed + state[2] * factor
    return top, total, summed


def chip_position(cut, group, place, core, rows):
    chip = lax.rem(group * GROUP + place + (cut + 2 * CHIPS), CHIPS)
    return (chip * 2 + core) * rows


def blocks_of(ref, low, high, offset=0):
    rows = ref.shape[2]
    return [ref[low:high, offset + i].reshape((high - low) * rows, HEAD_DIM) for i in range(2)]


def attend_kernel(long_chip, phase, starts, q_ref, *refs):
    cut, even = cut_of(long_chip)
    group, core = group_of(cut), lax.axis_index("core")
    rows = q_ref.shape[2]
    place = lax.broadcasted_iota(jnp.int32, (rows, 1), 0)

    is_even = lax.rem(group + even, 2) == 0

    def own(ref, of_core, count, offset=0):
        blocks = blocks_of(ref, 0, count, offset)
        return *blocks, [chip_position(cut, group, i, of_core, rows) for i in range(count)]

    def before(ref, of_core):
        first = [chip_position(cut, group - 1, i, of_core, rows) for i in range(GROUP)]
        return *blocks_of(ref, 0, GROUP), [jnp.where(is_even, -2 * LONG, here) for here in first]

    def edge(ref, of_core):
        back = jnp.where(is_even, 1, 2)
        return ref[0, 0], ref[0, 1], [chip_position(cut, group - back, GROUP - 1, of_core, rows)]

    if phase == 0:
        other, edge_ref, edge_other, *outs = refs
        sources = [own(q_ref, core, GROUP, 1), own(other, 1 - core, GROUP)]
        sources += [edge(edge_ref, core), edge(edge_other, 1 - core)]
    else:
        sources = [before(refs[0], core if phase == 1 else 1 - core)]
        state, outs = refs[1:4], refs[4:]

    @pl.loop(0, GROUP, unroll=2 if phase == 2 else 1)
    def _(block):
        query_first = chip_position(cut, group, block, core, rows)
        query_pos = query_first + place
        here = sources
        if phase > 0:
            ((keys, values, firsts),) = sources
            firsts = [jnp.where(first < query_first, first, -2 * LONG) for first in firsts]
            here = [(keys, values, firsts)]
        top, total, summed = attend_rows(
            q_ref[block, 0],
            query_pos,
            row_starts(starts, query_pos),
            here,
            None if phase == 0 else [ref[block] for ref in state],
            causal=phase == 0,
        )
        if phase < 2:
            outs[0][block], outs[1][block], outs[2][block] = top, total, summed
        else:
            outs[0][block] = summed / total


def attend(long_chip, phase, starts, received, *others):
    rows = received.shape[2]
    column = jax.ShapeDtypeStruct((GROUP, rows, 1), jnp.float32)
    full = jax.ShapeDtypeStruct((GROUP, rows, HEAD_DIM), jnp.float32)
    return pl.pallas_call(
        functools.partial(attend_kernel, long_chip, phase),
        out_shape=full if phase == 2 else (column, column, full),
        in_specs=[SMEM] + [VMEM] * (1 + len(others)),
        compiler_params=pltpu.CompilerParams(vmem_limit_bytes=32 * 1024 * 1024),
        cost_estimate=cost(2000 if phase else 10),
        name=f"attend{phase}",
    )(starts, received, *others)


def row_starts(starts, positions):
    found = jnp.zeros_like(positions)
    for record in range(starts.shape[0]):
        here = starts[record]
        found = jnp.where(positions >= here, here, found)
    return found


def hyena_kernel(starts, residual, streams, rim, taps_ref, out_ref, padded):
    rows = residual.shape[0]
    edge = rim.shape[1]
    taps = taps_ref.shape[0]
    positions = lax.axis_index(POSITIONS) * rows + lax.broadcasted_iota(jnp.int32, (rows, 1), 0)
    first = row_starts(starts, positions)
    padded[:edge] = rim[0].astype(jnp.float32) * rim[1].astype(jnp.float32)
    padded[edge:] = streams[1].astype(jnp.float32) * streams[2].astype(jnp.float32)
    filtered = jnp.zeros(out_ref.shape, jnp.float32)
    for tap in range(taps):
        term = taps_ref[tap : tap + 1, :] * padded[edge - tap : edge - tap + rows]
        filtered = filtered + jnp.where(positions - tap >= first, term, 0.0)
    out_ref[...] = residual[...].astype(jnp.float32) + streams[0].astype(jnp.float32) * filtered


def stream_kernel(base, heads, stream_ref, squares_ref):
    rows = base.shape[0]
    squares = jnp.zeros((rows, HEAD_DIM), jnp.float32)
    for head in range(GROUP):
        columns = slice(head * HEAD_DIM, (head + 1) * HEAD_DIM)
        value = base[:, columns] + heads[head]
        stream_ref[:, columns] = value
        squares = squares + value * value
    line = jnp.sum(squares.T, axis=0, keepdims=True)
    for device in range(squares_ref.shape[0]):
        squares_ref[device] = line


def records_kernel(lines, parts, mean_ref, sums_ref):
    rows = parts.shape[2]
    line = jnp.sum(parts[:, 0, :], axis=0, keepdims=True) / D
    mean = jnp.broadcast_to(line, (rows, rows)).T
    mean_ref[...] = mean
    position = lax.axis_index(POSITIONS) * rows + lax.broadcasted_iota(jnp.int32, (rows, rows), 0)
    first = lines[0]
    inside = (position >= first) & (position < first + lines[1])
    sums = jnp.sum(jnp.where(inside, mean, 0.0), axis=0, keepdims=True)
    for device in range(sums_ref.shape[0]):
        sums_ref[device] = sums


def scale_kernel(stream, mean, gain, out_ref):
    factor = lax.rsqrt(mean[...] + 1e-05)
    for head in range(GROUP):
        columns = slice(head * HEAD_DIM, (head + 1) * HEAD_DIM)
        out_ref[:, columns] = stream[:, columns] * factor * gain[:, columns]


def mixers(long_chip, packed, residual, streams, taps, starts):
    rows, width = residual.shape
    cut, even = cut_of(long_chip)
    seq = lax.axis_size(POSITIONS)
    groups = [
        [(cut + GROUP * k + i) % CHIPS for i in range(GROUP)] for k in range(CHIPS // GROUP)
    ]
    swap = [(0, 1), (1, 0)]

    def along(value, count, of_groups):
        pairs = [(i, (i + count * GROUP) % CHIPS) for k in of_groups for i in groups[k]]
        return lax.ppermute(value, "z", pairs)

    evens, odds = [even, even + 2], [1 - even, 3 - even]
    rim = lax.ppermute(streams[1:, rows - 16 :], POSITIONS, [(i, i + 1) for i in range(seq - 1)])
    received = lax.all_to_all(packed, "z", 0, 0, axis_index_groups=groups, tiled=True)
    key_value, rim = lax.optimization_barrier((received[:, 1:], rim))
    before = along(key_value, 1, evens)
    last = received[GROUP - 1 :, 1:]
    other = lax.ppermute(key_value, "core", swap)
    last, streams, other = lax.optimization_barrier((last, streams, other))
    edge = along(last, 2, odds) + along(last, 1, odds)
    base = pl.pallas_call(
        hyena_kernel,
        out_shape=jax.ShapeDtypeStruct((rows, width), jnp.float32),
        in_specs=[SMEM, VMEM, VMEM, VMEM, VMEM],
        out_specs=VMEM,
        scratch_shapes=[pltpu.VMEM((rows + 16, width), jnp.float32)],
        cost_estimate=cost(10),
        name="hyena",
    )(starts, residual, streams, rim, taps)
    edge_other = lax.ppermute(edge, "core", swap)
    state = attend(long_chip, 0, starts, received, other, edge, edge_other)
    before, state, base = lax.optimization_barrier((before, state, base))
    before_other = lax.ppermute(before, "core", swap)
    state = attend(long_chip, 1, starts, received, before, *state)
    out = attend(long_chip, 2, starts, received, before_other, *state)
    out = out.astype(jnp.float16)
    heads = lax.all_to_all(out, "z", 0, 0, axis_index_groups=groups, tiled=True)
    return base, heads.astype(jnp.float32)


def on_device(
    residual,
    hyena_streams,
    hyena_filter,
    attention_streams,
    norm_gain,
    record_starts,
    record_lengths,
    segment_ids,
):
    rows, width = residual.shape
    records = record_starts.shape[0]
    seq, mp = lax.axis_size(POSITIONS), lax.axis_size("mp")
    packed, lines, chip = pack(record_starts, record_lengths, attention_streams.transpose(1, 0, 2))
    base, heads = lax.switch(
        chip[0],
        [functools.partial(mixers, here) for here in range(CHIPS - LONG // (2 * rows) + 1)],
        packed,
        residual,
        hyena_streams.transpose(1, 0, 2),
        hyena_filter,
        record_starts,
    )

    with jax.named_scope("mean_square"):
        stream, squares = pl.pallas_call(
            stream_kernel,
            out_shape=(
                jax.ShapeDtypeStruct((rows, width), jnp.float32),
                jax.ShapeDtypeStruct((mp, 1, rows), jnp.float32),
            ),
            name="stream",
        )(base, heads)
        parts = lax.all_to_all(squares, "mp", 0, 0, tiled=True)
    with jax.named_scope("record_energy"):
        mean, sums = pl.pallas_call(
            records_kernel,
            out_shape=(
                jax.ShapeDtypeStruct((rows, rows), jnp.float32),
                jax.ShapeDtypeStruct((seq, 1, 128), jnp.float32),
            ),
            name="records",
        )(lines, parts)
        sums = lax.all_to_all(sums, POSITIONS, 0, 0, tiled=True)
        record_energy = jnp.sum(sums, axis=(0, 1))[:records] / record_lengths.astype(jnp.float32)
    mixed = pl.pallas_call(
        scale_kernel,
        out_shape=jax.ShapeDtypeStruct((rows, width), jnp.float32),
        cost_estimate=cost(1000),
        name="scale",
    )(stream, mean, norm_gain[None, :])
    return (mixed, record_energy)


def solution(mesh):
    fine = Mesh(mesh.devices.reshape(CHIPS, 2, mesh.shape["mp"]), ("z", "core", "mp"))
    return jax.shard_map(
        on_device,
        mesh=fine,
        in_specs=(
            P(POSITIONS, "mp"),
            P(POSITIONS, None, "mp"),
            P(None, "mp"),
            P(POSITIONS, None, "mp"),
            P("mp"),
            P(),
            P(),
            P(POSITIONS),
        ),
        out_specs=(P(POSITIONS, "mp"), P()),
        check_vma=False,
    )
```
